32 devices in a mesh: user: 8 (over z, y), item: 4 (over x, core).
Axes of the slice: x: 2, y: 2, z: 4, core: 2. Of those that a mesh axis runs over, the one named last changes fastest.
Arguments:
- item_init: float32 [4096, 128], P(('item', 'user')), may hold values from -1.8 to 1.8
- tile_rows: int32 [8, 4, 48], P('user', 'item'), may hold values from 0 to 7, as said below
- tile_cols: int32 [8, 4, 48], P('user', 'item'), may hold values from 0 to 7, as said below
- tile_count: int32 [8, 4], P('user', 'item'), may hold values from 24 to 48, as said below
- conf: int32 [8, 4, 48, 128, 128], P('user', 'item'), may hold values from 0 to 7, as said below
Outputs:
- user_factors: float32 [8192, 128], P(('user', 'item'))
- item_factors: float32 [4096, 128], P(('item', 'user'))
The draws below stay inside these ranges and needn't reach their ends.
Inputs may be any that keep to these rules, and one draw needn't show every extreme that they name: `tile_rows`: every user block of a group is named by a slot below 24 of some device of that group. `tile_cols`: slot t of device (u, i) names item block (t + s) mod 8, with s fixed for the device; every item block of a group is named by a slot below 24 of some device of that group; device (u, i) owns item block u of its group (item block i * 8 + u in all), and at most 6 slots of one device name blocks of one such device, exactly 6 for some. `tile_count`: some device uses all 48 slots. `conf`: the diagonal entries of every tile are nonzero.
All inputs are finite; a program needn't handle non-finite values.
Results may differ from the reference program's by a relative error of at most 0.0003.
Values sent between devices are 32-bit elements; how exact they have to be, the bound alone decides.
No kernel may reach another device: no remote copies, remote signals or barrier semaphores. Data moves between devices by JAX's collectives and lax.ppermute only.
A program may use at most 64 MiB of HBM per device.

```python
import jax
import jax.numpy as jnp
from jax import lax

K = 128
BS = 128
IB = 1
NT = 48
CG_ITERS = 3
USER_SHARDS = 8
ITEM_SHARDS = 4
ROW_BLOCKS = 8
COL_BLOCKS = 8
USERS = 8192
ITEMS = 4096
N_USER = 8


def draw_tile_rows(key, part):
    half_slots = NT // 2
    slot_index = jnp.arange(NT, dtype=jnp.int32)[None, None, :]
    shard_item = jnp.arange(ITEM_SHARDS, dtype=jnp.int32)[None, :, None]
    offsets = jax.random.randint(jax.random.fold_in(key, 11), (USER_SHARDS, 1, 1), 0, ROW_BLOCKS, dtype=jnp.int32)
    covered = (slot_index + half_slots * shard_item + offsets) % ROW_BLOCKS
    scattered = jax.random.randint(jax.random.fold_in(key, 12), (USER_SHARDS, ITEM_SHARDS, NT), 0, ROW_BLOCKS, dtype=jnp.int32)
    return jnp.where(slot_index < half_slots, covered, scattered).astype(jnp.int32)


def draw_tile_cols(key, part):
    half_slots = NT // 2
    run_steps = half_slots // IB
    slot_index = jnp.arange(NT, dtype=jnp.int32)[None, None, :]
    shard_user = jnp.arange(USER_SHARDS, dtype=jnp.int32)[:, None, None]
    offsets = jax.random.randint(jax.random.fold_in(key, 13), (1, ITEM_SHARDS, 1), 0, N_USER, dtype=jnp.int32)
    shifts = IB * (run_steps * shard_user + offsets)
    return ((slot_index + shifts) % COL_BLOCKS).astype(jnp.int32)


def draw_tile_count(key, part):
    device_total = USER_SHARDS * ITEM_SHARDS
    counts = jax.random.randint(jax.random.fold_in(key, 21), (device_total,), NT // 2, NT + 1, dtype=jnp.int32)
    fullest = jax.random.randint(jax.random.fold_in(key, 22), (), 0, device_total, dtype=jnp.int32)
    device_index = jnp.arange(device_total, dtype=jnp.int32)
    return jnp.where(device_index == fullest, NT, counts).reshape(USER_SHARDS, ITEM_SHARDS).astype(jnp.int32)


def draw_conf(key, part):
    array_shape = (USER_SHARDS, ITEM_SHARDS, NT, BS, BS)
    values = jax.random.randint(jax.random.fold_in(key, 31), array_shape, 1, 8, dtype=jnp.int32)
    chosen = jax.random.randint(jax.random.fold_in(key, 32), array_shape, 0, 16, dtype=jnp.int32) == 0
    diagonal = jnp.arange(BS)[:, None] == jnp.arange(BS)[None, :]
    return jnp.where(chosen | diagonal, values, 0).astype(jnp.int32)


def block_levels(stream_key, dims, shards, low, high):
    def one(dim, shards_of):
        steps = jax.random.uniform(jax.random.fold_in(jax.random.fold_in(stream_key, 6), dim), (shards_of,), jnp.float32, low / len(shards), high / len(shards))
        return jnp.repeat(jnp.exp(steps), dims[dim] // shards_of).reshape((-1,) + (1,) * (len(dims) - dim - 1))

    gain = one(*shards[0])
    for cut in shards[1:]:
        gain = gain * one(*cut)
    return gain


def normal_values(rng, shape, deviation, bound, shards=(), held_as=jnp.bfloat16):
    entries = deviation * jax.random.normal(rng, shape, jnp.float32)
    if shards:
        entries = entries * block_levels(rng, shape, shards, -0.22, 0.18)
    return jnp.clip(entries, -bound, bound).astype(held_as)


def setup_inputs(seed: int = 0) -> dict:
    key_of = jax.random.split(jax.random.key(seed), 6)
    return {
        "item_init": normal_values(key_of[0], (ITEMS, K), 0.3, 1.8, ((0, 32),), jnp.float32),
        "tile_rows": draw_tile_rows(jax.random.fold_in(key_of[5], 71), 0),
        "tile_cols": draw_tile_cols(jax.random.fold_in(key_of[5], 71), 0),
        "tile_count": draw_tile_count(jax.random.fold_in(key_of[5], 71), 0),
        "conf": draw_conf(jax.random.fold_in(key_of[5], 71), 0),
    }


highest = lax.Precision.HIGHEST
ridge = 5.0
unobserved = 256.0


def slot_products(own_blocks, other_blocks, tile_values, own_ids, other_ids):
    own_rows = jnp.take(own_blocks, own_ids, axis=0)
    other_rows = jnp.take(other_blocks, other_ids, axis=0)
    scores = jnp.einsum('tik,tjk->tij', own_rows, other_rows, precision=highest)
    return jnp.einsum('tij,tjk->tik', scores * tile_values, other_rows, precision=highest)


def conjugate(right_side, apply_operator):
    solution = jnp.zeros_like(right_side)
    residual = right_side
    direction = right_side
    norm_now = jnp.sum(residual * residual, axis=-1, keepdims=True)
    for iteration in range(CG_ITERS):
        product_vec = apply_operator(direction)
        step_length = norm_now / jnp.sum(direction * product_vec, axis=-1, keepdims=True)
        solution = solution + step_length * direction
        residual = residual - step_length * product_vec
        norm_next = jnp.sum(residual * residual, axis=-1, keepdims=True)
        direction = residual + (norm_next / norm_now) * direction
        norm_now = norm_next
    return solution


def half_step(other_factors, own_count, slot_data, transpose):
    other_blocks = other_factors.reshape(-1, BS, K)
    gram = jnp.dot(other_factors.T, other_factors, precision=highest)
    weight_zero = unobserved / other_factors.shape[0]

    def accumulate(make_terms):
        def scan_step(summed, inputs):
            counts, row_ids, col_ids, usable = inputs
            slot_mask = usable[:, None, None]
            counts_float = counts.astype(jnp.float32)
            confidence = jnp.where(slot_mask, counts_float, jnp.float32(0.0))
            weights = jnp.where(slot_mask & (counts > 0), 1.0 + counts_float, jnp.float32(0.0))
            own_ids, other_ids = row_ids, col_ids
            if transpose:
                confidence = jnp.swapaxes(confidence, 1, 2)
                weights = jnp.swapaxes(weights, 1, 2)
                own_ids, other_ids = col_ids, row_ids
            terms = make_terms(confidence, weights, own_ids, other_ids)
            return summed.at[own_ids].add(terms), None

        summed, unused = lax.scan(scan_step, jnp.zeros((own_count, BS, K), jnp.float32), slot_data)
        return summed.reshape(own_count * BS, K)

    def side_terms(confidence, weights, own_ids, other_ids):
        return jnp.einsum('tij,tjk->tik', weights, jnp.take(other_blocks, other_ids, axis=0), precision=highest)

    right_side = accumulate(side_terms)

    def apply_operator(direction):
        dir_blocks = direction.reshape(-1, BS, K)

        def product_terms(confidence, weights, own_ids, other_ids):
            return slot_products(dir_blocks, other_blocks, confidence, own_ids, other_ids)

        tile_part = accumulate(product_terms)
        return tile_part + weight_zero * jnp.dot(direction, gram, precision=highest) + ridge * direction

    return conjugate(right_side, apply_operator)


def reference(item_init, tile_rows, tile_cols, tile_count, conf):
    user_index = jnp.arange(USER_SHARDS, dtype=jnp.int32)[:, None, None]
    item_index = jnp.arange(ITEM_SHARDS, dtype=jnp.int32)[None, :, None]
    row_ids = (user_index * ROW_BLOCKS + tile_rows).reshape(-1, NT).astype(jnp.int32)
    col_ids = (item_index * COL_BLOCKS + tile_cols).reshape(-1, NT).astype(jnp.int32)
    usable = (jnp.arange(NT, dtype=jnp.int32)[None, None, :] < tile_count[:, :, None]).reshape(-1, NT)
    slot_data = (conf.reshape(-1, NT, BS, BS), row_ids, col_ids, usable)
    user_factors = half_step(item_init, USERS // BS, slot_data, False)
    item_factors = half_step(user_factors, ITEMS // BS, slot_data, True)
    return user_factors, item_factors
```

```python
import functools

import jax
import jax.numpy as jnp
from jax import lax
from jax.experimental import pallas as pl
from jax.experimental.pallas import tpu as pltpu
from jax.sharding import PartitionSpec as P

UB = 2
IB = 1
CG_ITERS = 3


highest = lax.Precision.HIGHEST
ridge = 5.0
unobserved = 256.0

f32 = jnp.float32
bf16 = jnp.bfloat16
MIB = 1 << 20
DENSE_LIMIT = 8 * MIB


def pair(value):
    high = value.astype(bf16)
    low = (value - high.astype(f32)).astype(bf16)
    return high, low


def row_sum(value):
    return jnp.sum(value, axis=-1, keepdims=True)


def split_rows(value):
    high, low = pair(value)
    return jnp.concatenate(
        [jnp.concatenate([high, low], axis=1), jnp.concatenate([low, high], axis=1)], axis=0
    )


def scores_of(lhs, factors):
    rows = lhs.shape[0] // 2
    both = lax.dot_general(lhs, factors, (((1,), (1,)), ((), ())), preferred_element_type=f32)
    return both[:rows] + both[rows:]


def tile_terms(direction, conf_ref, pairs_ref, width):
    rows, rank = direction.shape
    lhs = split_rows(direction)
    total = jnp.zeros((rows, rank), f32)
    for start in range(0, conf_ref.shape[1], width):
        factors = pairs_ref[start : start + width, :]
        weighted = scores_of(lhs, factors) * conf_ref[:, start : start + width]
        high, low = pair(weighted)
        out = jnp.dot(jnp.concatenate([high, low], axis=0), factors, preferred_element_type=f32)
        total = total + (
            (out[:rows, :rank] + out[:rows, rank:]) + (out[rows:, :rank] + out[rows:, rank:])
        )
    return total


def tile_squares(direction, conf_ref, pairs_ref, width):
    rows, rank = direction.shape
    lhs = split_rows(direction)
    total = jnp.zeros((rows, rank), f32)
    for start in range(0, conf_ref.shape[1], width):
        scores = scores_of(lhs, pairs_ref[start : start + width, :])
        squares = scores * scores * conf_ref[:, start : start + width]
        for part in range(0, width, rank):
            total = total + squares[:, part : part + rank]
    return total


def side_of(weight_ref, pairs_ref):
    rank = pairs_ref.shape[1] // 2
    both = jnp.dot(weight_ref[...], pairs_ref[...], preferred_element_type=f32)
    return both[:, :rank] + both[:, rank:]


def advance(solution, residual, direction, product):
    norm_now = row_sum(residual * residual)
    step_length = norm_now / row_sum(direction * product)
    solution = solution + step_length * direction
    residual = residual - step_length * product
    direction = residual + row_sum(residual * residual) / norm_now * direction
    return solution, residual, direction


def pack_kernel(slots, ids_ref, conf_ref, send_ref):
    slot_total, block, _ = conf_ref.shape
    owners = send_ref.shape[0]
    shift = ids_ref[slot_total]
    count = ids_ref[2 * slot_total]

    def one(owner, carry):
        first = lax.rem(owner - shift + owners, owners)
        for slot in range(slots):
            place = first + owners * slot
            used = place < jnp.minimum(count, slot_total)
            held = jnp.minimum(place, slot_total - 1)
            send_ref[owner, slot * block : (slot + 1) * block, :] = jnp.where(used, conf_ref[held], 0)
            send_ref[owner, slots * block + slot, :] = jnp.full((block,), ids_ref[held], jnp.int32)
        return carry

    lax.fori_loop(0, owners, one, 0)


def user_tiles_kernel(weight_zero, own_ids, other_ids, conf_ref, half_ref, dense_ref, weight_ref):
    slot_total, block, _ = conf_ref.shape
    half = block // 2
    owners = dense_ref.shape[1] // block // 2
    me = lax.axis_index("user")
    core = lax.rem(lax.axis_index("item"), 2)
    dense_ref[...] = jnp.full(dense_ref.shape, weight_zero, f32)
    weight_ref[...] = jnp.zeros(weight_ref.shape, bf16)

    def place(ids, slot, base, counts):
        row = pl.multiple_of(ids[slot] * half, half)
        col = pl.multiple_of((base + jnp.bitwise_xor(ids[slot_total + slot], me)) * block, block)
        at = (pl.ds(row, half), pl.ds(col, block))
        value = counts.astype(f32)
        dense_ref[at] = dense_ref[at] + value
        weight_ref[at] = weight_ref[at] + jnp.where(value > 0.0, 1.0 + value, 0.0).astype(bf16)

    def own(slot, carry):
        rows = pl.ds(pl.multiple_of(core * half, half), half)
        place(own_ids, slot, 0, conf_ref[slot, rows, :])
        return carry

    def other(slot, carry):
        place(other_ids, slot, owners, half_ref[slot])
        return carry

    lax.fori_loop(0, jnp.minimum(own_ids[2 * slot_total], slot_total), own, 0)
    lax.fori_loop(0, jnp.minimum(other_ids[2 * slot_total], slot_total), other, 0)


def user_side_kernel(count, *refs):
    pieces, (weight_ref, side_ref, pairs_ref) = refs[:count], refs[count:]
    start = 0
    for piece in pieces:
        flat = piece[...].reshape(-1, piece.shape[-1])
        high, low = pair(flat)
        pairs_ref[start : start + flat.shape[0], :] = jnp.concatenate([high, low], axis=1)
        start += flat.shape[0]
    side_ref[...] = side_of(weight_ref, pairs_ref)


def user_first_kernel(width, own_ref, other_ref, conf_ref, pairs_ref, side_ref, out_ref):
    side = own_ref[...] + other_ref[...]
    side_ref[...] = side
    out_ref[...] = tile_terms(side, conf_ref, pairs_ref, width)


def user_second_kernel(
    width, side_ref, own_ref, other_ref, conf_ref, pairs_ref, x_ref, r_ref, d_ref, out_ref
):
    side = side_ref[...]
    product = own_ref[...] + other_ref[...] + ridge * side
    x, r, d = advance(jnp.zeros_like(side), side, side, product)
    x_ref[...] = x
    r_ref[...] = r
    d_ref[...] = d
    out_ref[...] = tile_terms(d, conf_ref, pairs_ref, width)


def user_third_kernel(
    width, x_in, r_in, d_in, own_ref, other_ref, conf_ref, pairs_ref, x_ref, r_ref, d_ref, sums_ref
):
    direction = d_in[...]
    product = own_ref[...] + other_ref[...] + ridge * direction
    x, r, d = advance(x_in[...], r_in[...], direction, product)
    x_ref[...] = x
    r_ref[...] = r
    d_ref[...] = d
    squares = tile_squares(d, conf_ref, pairs_ref, width)
    ones = jnp.ones((8, squares.shape[1]), bf16)
    sums = jnp.zeros(sums_ref.shape, f32)
    for unused in range(3):
        part = squares.astype(bf16)
        squares = squares - part.astype(f32)
        sums = sums + lax.dot_general(ones, part, (((1,), (1,)), ((), ())), preferred_element_type=f32)
    sums_ref[...] = sums


def user_last_kernel(blocks, x_in, r_in, d_in, own_ref, other_ref, out_ref, keep_ref, give_ref):
    place = lax.axis_index("item")
    residual = r_in[...]
    direction = d_in[...]
    sums = jnp.transpose(own_ref[...] + other_ref[...])[:, :1]
    length = row_sum(residual * residual) / (sums + ridge * row_sum(direction * direction))
    out_ref[...] = x_in[...] + length * direction
    rows = keep_ref.shape[0]
    keep_ref[...] = out_ref[pl.ds(pl.multiple_of(place * rows, rows), rows), :]
    other = jnp.bitwise_xor(place, 1)
    give_ref[...] = out_ref[pl.ds(pl.multiple_of(other * rows, rows), rows), :]


def item_tiles_kernel(weight_zero, slots, row_blocks, ids_ref, tiles_ref, dense_ref, weight_ref):
    owners = tiles_ref.shape[0]
    block = tiles_ref.shape[2]
    me = lax.axis_index("user")
    dense_ref[...] = jnp.full(dense_ref.shape, weight_zero, f32)
    weight_ref[...] = jnp.zeros(weight_ref.shape, bf16)

    def one(source, carry):
        base = jnp.bitwise_xor(source, me) * row_blocks
        for slot in range(slots):
            value = jnp.transpose(tiles_ref[source, slot * block : (slot + 1) * block, :].astype(f32))
            col = pl.multiple_of((base + ids_ref[source * slots + slot]) * block, block)
            at = (slice(None), pl.ds(col, block))
            dense_ref[at] = dense_ref[at] + value
            weight_ref[at] = weight_ref[at] + jnp.where(value > 0.0, 1.0 + value, 0.0).astype(bf16)
        return carry

    lax.fori_loop(0, owners, one, 0)


def item_kernel(width, row_blocks, *refs):
    pieces, (conf_ref, weight_ref, out_ref, pairs_ref) = refs[:-4], refs[-4:]
    block = out_ref.shape[0]
    half = block // 2
    core = lax.rem(lax.axis_index("item"), 2)
    group = 0
    for own_half, piece in pieces_in_order(pieces):
        offset = pl.multiple_of((core if own_half else 1 - core) * half, half)
        for row in range(row_blocks):
            high, low = pair(piece[row * half : (row + 1) * half, :])
            pairs_ref[pl.ds((group // 2 * row_blocks + row) * block + offset, half), :] = (
                jnp.concatenate([high, low], axis=1)
            )
        group += 1
    side = side_of(weight_ref, pairs_ref)
    x, r, d = jnp.zeros_like(side), side, side
    for unused in range(CG_ITERS - 1):
        product = tile_terms(d, conf_ref, pairs_ref, width) + ridge * d
        x, r, d = advance(x, r, d, product)
    bottom = row_sum(tile_squares(d, conf_ref, pairs_ref, width)) + ridge * row_sum(d * d)
    out_ref[...] = x + row_sum(r * r) / bottom * d


def pieces_in_order(pieces):
    return [(place % 2 == 0, piece) for place, piece in enumerate(pieces)]


VMEM = pltpu.VMEM
SMEM = pltpu.SMEM


def call(kernel, outs, *operands, scalars=0, flops=0, scratch=(), limit=48):
    size = sum(op.size * op.dtype.itemsize for op in operands)
    size += sum(out.size * out.dtype.itemsize for out in outs)
    spaces = [SMEM] * scalars + [VMEM] * (len(operands) - scalars)
    return pl.pallas_call(
        kernel,
        out_shape=tuple(outs),
        in_specs=[pl.BlockSpec(memory_space=space) for space in spaces],
        out_specs=tuple(pl.BlockSpec(memory_space=VMEM) for unused in outs),
        scratch_shapes=scratch,
        compiler_params=pltpu.CompilerParams(vmem_limit_bytes=limit * MIB),
        cost_estimate=pl.CostEstimate(flops=flops, bytes_accessed=size, transcendentals=0),
    )(*operands)


def shaped(shape, dtype=f32):
    return jax.ShapeDtypeStruct(shape, dtype)


def dense_shards(item_init, tile_rows, tile_cols, tile_count, conf):
    slot_total = tile_rows.shape[-1]
    block, rank = conf.shape[-1], item_init.shape[1]
    half = block // 2
    n_item, n_user = lax.axis_size("item"), lax.axis_size("user")
    row_blocks = UB * n_item
    rows = row_blocks * half
    slots = -(-slot_total // n_user)
    width = 2 * rank
    me = lax.axis_index("item")
    core = lax.rem(me, 2)

    def swap(value, axis, mask):
        size = n_item if axis == "item" else n_user
        return lax.ppermute(value, axis, [(place, place ^ mask) for place in range(size)])

    def others(value):
        total = value
        mask = 2
        while mask < n_item:
            moved = swap(total, "item", mask)
            if mask * 2 >= n_item:
                return total, moved
            total = total + moved
            mask *= 2

    conf = conf.reshape(slot_total, block, block)
    ids = jnp.concatenate(
        [tile_rows.reshape(-1), tile_cols.reshape(-1), tile_count.reshape(-1)]
    ).astype(jnp.int32)

    with jax.named_scope("gather_items"):
        pieces = {0: item_init, 1: swap(item_init, "user", 1)}
        for mask in range(2, n_user, 2):
            pieces[mask] = swap(item_init, "user", mask)
        for mask in range(2, n_user, 2):
            pieces[mask + 1] = swap(pieces[mask], "user", 1)
        own_items = jnp.stack([pieces[mask] for mask in range(n_user)])
        other_items = swap(own_items, "item", 1)

    with jax.named_scope("user_tiles"):
        other_ids = swap(ids, "item", 1)
        given = lax.dynamic_slice(conf, (0, (1 - core) * half, 0), (slot_total, half, block))
        other_half = swap(given, "item", 1)
        columns = 2 * n_user * block
        user_conf, user_weight = call(
            functools.partial(user_tiles_kernel, unobserved / (item_init.shape[0] * n_user * n_item)),
            (shaped((rows, columns)), shaped((rows, columns), bf16)),
            ids, other_ids, conf, other_half, scalars=2, flops=10 ** 9,
        )

    with jax.named_scope("send_tiles"):
        tied_ids, tied_conf, own_items = lax.optimization_barrier((ids, conf, own_items))
        (packed,) = call(
            functools.partial(pack_kernel, slots),
            (shaped((n_user, slots * block + 8, block), jnp.int32),),
            tied_ids, tied_conf, scalars=1, flops=10 ** 9,
        )
        item_tiles = lax.all_to_all(packed, "user", 0, 0, tiled=True)

    cost = 2 * rows * columns * rank
    state = shaped((rows, rank))
    with jax.named_scope("user_cg"):
        part, pairs = call(
            functools.partial(user_side_kernel, 2),
            (state, shaped((columns, 2 * rank), bf16)),
            own_items, other_items, user_weight, flops=2 * cost,
        )
        side, part = call(
            functools.partial(user_first_kernel, width), (state, state),
            *others(part), user_conf, pairs, flops=6 * cost,
        )
        x, r, d, part = call(
            functools.partial(user_second_kernel, width), (state,) * 4,
            side, *others(part), user_conf, pairs, flops=6 * cost,
        )
        x, r, d, sums = call(
            functools.partial(user_third_kernel, width), (state,) * 3 + (shaped((8, rows)),),
            x, r, d, *others(part), user_conf, pairs, flops=3 * cost,
        )
        shard = shaped((UB * half, rank))
        users, keep, give = call(
            functools.partial(user_last_kernel, row_blocks), (state, shard, shard),
            x, r, d, *others(sums), flops=10 ** 6,
        )
        taken = swap(give, "item", 1)
        keep, taken = keep.reshape(UB, half, rank), taken.reshape(UB, half, rank)
        user_factors = jnp.stack(
            [jnp.where(core == 0, keep, taken), jnp.where(core == 0, taken, keep)], axis=1
        ).reshape(UB * block, rank)

    with jax.named_scope("gather_users"):
        pieces = {0: users, 1: swap(users, "user", 1)}
        for mask in range(2, n_user, 2):
            pieces[mask] = swap(users, "user", mask)
        for mask in range(2, n_user, 2):
            pieces[mask + 1] = swap(pieces[mask], "user", 1)
        ordered = []
        for mask in range(n_user):
            ordered += [pieces[mask], swap(pieces[mask], "item", 1)]

    with jax.named_scope("item_half"):
        row_ids = item_tiles[:, slots * block : slots * block + slots, 0].reshape(-1)
        columns = n_user * row_blocks * block
        item_conf, item_weight = call(
            functools.partial(
                item_tiles_kernel, unobserved / (user_factors.shape[0] * n_user * n_item), slots, row_blocks
            ),
            (shaped((block, columns)), shaped((block, columns), bf16)),
            row_ids, item_tiles, scalars=1, flops=10 ** 9,
        )
        (item_factors,) = call(
            functools.partial(item_kernel, width, row_blocks),
            (shaped((block, rank)),),
            *ordered, item_conf, item_weight, flops=20 * 2 * block * columns * rank,
            scratch=(pltpu.VMEM((columns, 2 * rank), bf16),),
        )
    return (user_factors, item_factors)


def fits_dense(mesh):
    n_user, n_item = mesh.shape["user"], mesh.shape["item"]
    block = 128
    user_bytes = UB * n_item * block * n_user * block * 4
    return user_bytes <= DENSE_LIMIT and n_item % 2 == 0 and n_user % 2 == 0


def block_sum(slot_terms, block_ids, row_count, block_size):
    block_count = row_count // block_size
    targets = jnp.arange(block_count, dtype=jnp.int32)
    onehot = (block_ids[:, None] == targets[None, :]).astype(jnp.float32)
    summed = jnp.einsum("tr,tik->rik", onehot, slot_terms, precision=highest)
    return summed.reshape(row_count, slot_terms.shape[2])


def group_products(own_blocks, other_blocks, tile_values, own_ids, other_ids):
    own_rows = jnp.take(own_blocks, own_ids, axis=0)
    other_rows = jnp.take(other_blocks, other_ids, axis=0)
    scores = jnp.einsum("tik,tjk->tij", own_rows, other_rows, precision=highest)
    return jnp.einsum("tij,tjk->tik", scores * tile_values, other_rows, precision=highest)


def slot_products(own_blocks, other_blocks, tile_values, own_ids, other_ids):
    return group_products(own_blocks, other_blocks, tile_values, own_ids, other_ids)


def conjugate(right_side, apply_operator):
    solution = jnp.zeros_like(right_side)
    residual = right_side
    direction = right_side
    norm_now = jnp.sum(residual * residual, axis=-1, keepdims=True)
    for iteration in range(CG_ITERS):
        product_vec = apply_operator(direction)
        step_length = norm_now / jnp.sum(direction * product_vec, axis=-1, keepdims=True)
        solution = solution + step_length * direction
        residual = residual - step_length * product_vec
        norm_next = jnp.sum(residual * residual, axis=-1, keepdims=True)
        direction = residual + norm_next / norm_now * direction
        norm_now = norm_next
    return solution


def shards(item_init, tile_rows, tile_cols, tile_count, conf):
    slot_total = tile_rows.shape[-1]
    block_size = conf.shape[-1]
    factor_rank = item_init.shape[1]
    item_devices = lax.axis_size("item")
    user_devices = lax.axis_size("user")
    row_ids = tile_rows.reshape(slot_total)
    col_ids = tile_cols.reshape(slot_total)
    slot_count = tile_count.reshape(())
    counts = conf.reshape(slot_total, block_size, block_size).astype(jnp.float32)
    usable = (jnp.arange(slot_total, dtype=jnp.int32) < slot_count)[:, None, None]
    confidence = jnp.where(usable, counts, 0.0)
    weights = jnp.where(usable & (counts > 0.0), 1.0 + counts, 0.0)
    user_rows = UB * block_size
    item_rows = IB * block_size
    item_shard = lax.all_gather(item_init, "user", axis=0, tiled=True)
    item_blocks = item_shard.reshape(-1, block_size, factor_rank)
    item_gram = lax.psum(jnp.dot(item_init.T, item_init, precision=highest), ("user", "item"))
    user_weight = unobserved / (item_init.shape[0] * user_devices * item_devices)
    user_terms = jnp.einsum(
        "tij,tjk->tik", weights, jnp.take(item_blocks, col_ids, axis=0), precision=highest
    )
    user_side = lax.psum_scatter(
        block_sum(user_terms, row_ids, user_rows * lax.axis_size("item"), block_size),
        "item",
        scatter_dimension=0,
        tiled=True,
    )

    def user_operator(direction):
        shard_direction = lax.all_gather(direction, "item", axis=0, tiled=True)
        slot_terms = slot_products(
            shard_direction.reshape(-1, block_size, factor_rank),
            item_blocks,
            confidence,
            row_ids,
            col_ids,
        )
        summed = lax.psum_scatter(
            block_sum(slot_terms, row_ids, user_rows * lax.axis_size("item"), block_size),
            "item",
            scatter_dimension=0,
            tiled=True,
        )
        return (
            summed
            + user_weight * jnp.dot(direction, item_gram, precision=highest)
            + ridge * direction
        )

    user_factors = conjugate(user_side, user_operator)
    user_shard = lax.all_gather(user_factors, "item", axis=0, tiled=True)
    user_blocks = user_shard.reshape(-1, block_size, factor_rank)
    user_gram = lax.psum(jnp.dot(user_factors.T, user_factors, precision=highest), ("user", "item"))
    item_weight = unobserved / (user_factors.shape[0] * user_devices * item_devices)
    confidence_cols = jnp.swapaxes(confidence, 1, 2)
    slot_users = jnp.take(user_blocks, row_ids, axis=0)
    item_terms = jnp.einsum("tij,tik->tjk", weights, slot_users, precision=highest)
    item_side = lax.psum_scatter(
        block_sum(item_terms, col_ids, item_rows * lax.axis_size("user"), block_size),
        "user",
        scatter_dimension=0,
        tiled=True,
    )

    def item_operator(direction):
        shard_direction = lax.all_gather(direction, "user", axis=0, tiled=True)
        slot_terms = slot_products(
            shard_direction.reshape(-1, block_size, factor_rank),
            user_blocks,
            confidence_cols,
            col_ids,
            row_ids,
        )
        summed = lax.psum_scatter(
            block_sum(slot_terms, col_ids, item_rows * lax.axis_size("user"), block_size),
            "user",
            scatter_dimension=0,
            tiled=True,
        )
        return (
            summed
            + item_weight * jnp.dot(direction, user_gram, precision=highest)
            + ridge * direction
        )

    item_factors = conjugate(item_side, item_operator)
    return (user_factors, item_factors)


def solution(mesh):
    in_specs = (
        P(("item", "user"), None),
        P("user", "item", None),
        P("user", "item", None),
        P("user", "item"),
        P("user", "item", None, None, None),
    )
    out_specs = (P(("user", "item"), None), P(("item", "user"), None))
    program = dense_shards if fits_dense(mesh) else shards
    return jax.shard_map(program, mesh=mesh, in_specs=in_specs, out_specs=out_specs, check_vma=False)
```

```python
import functools
import math

import jax
import jax.numpy as jnp
from jax import lax
from jax.experimental import pallas as pl
from jax.experimental.pallas import tpu as pltpu
from jax.sharding import PartitionSpec as P

UB = 2
IB = 1
CG_ITERS = 3
CHUNKS = 2


highest = lax.Precision.HIGHEST
ridge = 5.0
unobserved = 256.0

f32 = jnp.float32
bf16 = jnp.bfloat16
MIB = 1 << 20
DENSE_LIMIT = 8 * MIB


def pair(value):
    high = value.astype(bf16)
    low = (value - high.astype(f32)).astype(bf16)
    return high, low


def row_sum(value):
    return jnp.sum(value, axis=-1, keepdims=True)


def split_rows(value):
    high, low = pair(value)
    return jnp.concatenate(
        [jnp.concatenate([high, low], axis=1), jnp.concatenate([low, high], axis=1)], axis=0
    )


def scores_of(lhs, factors):
    rows = lhs.shape[0] // 2
    both = lax.dot_general(lhs, factors, (((1,), (1,)), ((), ())), preferred_element_type=f32)
    return both[:rows] + both[rows:]


def tile_terms(direction, conf_ref, pairs_ref, width, begin):
    rows, rank = direction.shape
    lhs = split_rows(direction)
    total = jnp.zeros((rows, rank), f32)
    for start in range(0, conf_ref.shape[1], width):
        factors = pairs_ref[start : start + width, :]
        weighted = scores_of(lhs, factors) * conf_ref[begin : begin + rows, start : start + width]
        high, low = pair(weighted)
        out = jnp.dot(jnp.concatenate([high, low], axis=0), factors, preferred_element_type=f32)
        total = total + (
            (out[:rows, :rank] + out[:rows, rank:]) + (out[rows:, :rank] + out[rows:, rank:])
        )
    return total


def tile_squares(direction, conf_ref, pairs_ref, width, begin):
    rows, rank = direction.shape
    lhs = split_rows(direction)
    total = jnp.zeros((rows, rank), f32)
    for start in range(0, conf_ref.shape[1], width):
        scores = scores_of(lhs, pairs_ref[start : start + width, :])
        squares = scores * scores * conf_ref[begin : begin + rows, start : start + width]
        for part in range(0, width, rank):
            total = total + squares[:, part : part + rank]
    return total


def write_sides(weight_ref, pairs_ref, side_refs):
    rank = pairs_ref.shape[1] // 2
    both = jnp.dot(weight_ref[...], pairs_ref[...], preferred_element_type=f32)
    start = 0
    for side_ref in side_refs:
        rows = slice(start, start + side_ref.shape[0])
        side_ref[...] = both[rows, :rank] + both[rows, rank:]
        start += side_ref.shape[0]


def advance(solution, residual, direction, product):
    norm_now = row_sum(residual * residual)
    step_length = norm_now / row_sum(direction * product)
    solution = solution + step_length * direction
    residual = residual - step_length * product
    direction = residual + row_sum(residual * residual) / norm_now * direction
    return solution, residual, direction


def pack_kernel(slots, ids_ref, conf_ref, given_ref, send_ref):
    slot_total, block, _ = conf_ref.shape
    half = block // 2
    owners = slot_total // slots
    near = owners // 2
    core = lax.rem(lax.axis_index("item"), 2)
    shift = ids_ref[slot_total]
    count = ids_ref[2 * slot_total]
    given_ref[...] = conf_ref[:, pl.ds(pl.multiple_of((1 - core) * half, half), half), :]
    for owner in range(owners):
        first = lax.rem(owner - shift + owners, owners)
        for slot in range(slots):
            place = first + owners * slot
            used = place < jnp.minimum(count, slot_total)
            send_ref[owner % near, owner // near * slots + slot] = jnp.where(used, conf_ref[place], 0)


def user_tiles_kernel(weight_zero, own_ids, other_ids, conf_ref, half_ref, dense_ref, weight_ref):
    slot_total, block, _ = conf_ref.shape
    half = block // 2
    owners = dense_ref.shape[1] // block // 2
    me = lax.axis_index("user")
    core = lax.rem(lax.axis_index("item"), 2)
    dense_ref[...] = jnp.full(dense_ref.shape, weight_zero, f32)
    weight_ref[...] = jnp.zeros(weight_ref.shape, bf16)

    def place(ids, slot, base, counts):
        row = pl.multiple_of(ids[slot] * half, half)
        col = pl.multiple_of((base + jnp.bitwise_xor(ids[slot_total + slot], me)) * block, block)
        at = (pl.ds(row, half), pl.ds(col, block))
        value = counts.astype(f32)
        dense_ref[at] = dense_ref[at] + value
        weight_ref[at] = weight_ref[at] + jnp.where(value > 0.0, 1.0 + value, 0.0).astype(bf16)

    def own(slot, carry):
        rows = pl.ds(pl.multiple_of(core * half, half), half)
        place(own_ids, slot, 0, conf_ref[slot, rows, :])
        return carry

    def other(slot, carry):
        place(other_ids, slot, owners, half_ref[slot])
        return carry

    lax.fori_loop(0, jnp.minimum(own_ids[2 * slot_total], slot_total), own, 0)
    lax.fori_loop(0, jnp.minimum(other_ids[2 * slot_total], slot_total), other, 0)


def user_side_kernel(count, *refs):
    pieces, (weight_ref, *side_refs, pairs_ref) = refs[:count], refs[count:]
    block = pairs_ref.shape[0] // count
    for place, piece in enumerate(pieces):
        high, low = pair(piece[:block, :])
        pairs_ref[place * block : (place + 1) * block, :] = jnp.concatenate([high, low], axis=1)
    write_sides(weight_ref, pairs_ref, side_refs)


def first_kernel(width, begin, own_ref, other_ref, conf_ref, pairs_ref, side_ref, out_ref):
    side = own_ref[...] + other_ref[...]
    side_ref[...] = side
    out_ref[...] = tile_terms(side, conf_ref, pairs_ref, width, begin)


def second_kernel(
    width, begin, side_ref, own_ref, other_ref, conf_ref, pairs_ref, x_ref, r_ref, d_ref, out_ref
):
    side = side_ref[...]
    product = own_ref[...] + other_ref[...] + ridge * side
    x, r, d = advance(jnp.zeros_like(side), side, side, product)
    x_ref[...] = x
    r_ref[...] = r
    d_ref[...] = d
    out_ref[...] = tile_terms(d, conf_ref, pairs_ref, width, begin)


def third_kernel(
    width, begin, x_in, r_in, d_in, own_ref, other_ref, conf_ref, pairs_ref, x_ref, r_ref, d_ref, sums_ref
):
    direction = d_in[...]
    product = own_ref[...] + other_ref[...] + ridge * direction
    x, r, d = advance(x_in[...], r_in[...], direction, product)
    x_ref[...] = x
    r_ref[...] = r
    d_ref[...] = d
    squares = tile_squares(d, conf_ref, pairs_ref, width, begin)
    ones = jnp.ones((8, squares.shape[1]), bf16)
    sums = jnp.zeros(sums_ref.shape, f32)
    for unused in range(3):
        part = squares.astype(bf16)
        squares = squares - part.astype(f32)
        sums = sums + lax.dot_general(ones, part, (((1,), (1,)), ((), ())), preferred_element_type=f32)
    sums_ref[...] = sums


def solve(refs, out_ref):
    start = 0
    for place in range(0, len(refs), 5):
        x_in, r_in, d_in, own_ref, other_ref = refs[place : place + 5]
        residual, direction = r_in[...], d_in[...]
        sums = jnp.transpose(own_ref[...] + other_ref[...])[:, :1]
        length = row_sum(residual * residual) / (sums + ridge * row_sum(direction * direction))
        out_ref[start : start + residual.shape[0], :] = x_in[...] + length * direction
        start += residual.shape[0]


def user_last_kernel(*refs):
    out_ref, keep_ref, give_ref = refs[-3:]
    solve(refs[:-3], out_ref)
    place = lax.axis_index("item")
    rows = keep_ref.shape[0]
    keep_ref[...] = out_ref[pl.ds(pl.multiple_of(place * rows, rows), rows), :]
    other = jnp.bitwise_xor(place, 1)
    give_ref[...] = out_ref[pl.ds(pl.multiple_of(other * rows, rows), rows), :]


def item_tiles_kernel(weight_zero, row_blocks, lists_ref, tiles_ref, dense_ref, weight_ref, token_ref):
    near, count, block, _ = tiles_ref.shape
    slots = count // 2
    me = lax.rem(lax.axis_index("user"), near)
    token_ref[...] = jnp.zeros(token_ref.shape, f32)
    dense_ref[...] = jnp.full(dense_ref.shape, weight_zero, f32)
    weight_ref[...] = jnp.zeros(weight_ref.shape, bf16)
    for source in range(near):
        mask = jnp.bitwise_xor(source, me)
        for upper in range(2):
            first = lax.rem(me + upper * near - lists_ref[mask, 1, 0] + 2 * near, 2 * near)
            for slot in range(slots):
                value = jnp.transpose(tiles_ref[source, upper * slots + slot].astype(f32))
                row = lists_ref[mask, 0, first + 2 * near * slot]
                col = pl.multiple_of((mask * row_blocks + row) * block, block)
                at = (slice(upper * block, (upper + 1) * block), pl.ds(col, block))
                dense_ref[at] = dense_ref[at] + value
                weight_ref[at] = weight_ref[at] + jnp.where(value > 0.0, 1.0 + value, 0.0).astype(bf16)


def join_kernel(block, own_ref, other_ref, out_ref):
    half = block // 2
    core = lax.rem(lax.axis_index("item"), 2)
    for start in range(0, out_ref.shape[0], block):
        for offset, part_ref in ((core, own_ref), (1 - core, other_ref)):
            rows = pl.ds(pl.multiple_of(start + offset * half, half), half)
            out_ref[rows, :] = part_ref[start // 2 : start // 2 + half, :]


def item_side_kernel(row_blocks, block, marks, *refs):
    pieces, (weight_ref, *side_refs, pairs_ref) = refs[: len(marks)], refs[len(marks) :]
    half = block // 2
    core = lax.rem(lax.axis_index("item"), 2)
    for (mask, own_half), piece in zip(marks, pieces):
        offset = pl.multiple_of((core if own_half else 1 - core) * half, half)
        for row in range(row_blocks):
            high, low = pair(piece[row * half : (row + 1) * half, :])
            start = (mask * row_blocks + row) * block
            pairs_ref[pl.ds(start + offset, half), :] = jnp.concatenate([high, low], axis=1)
    write_sides(weight_ref, pairs_ref, side_refs)


def item_last_kernel(*refs):
    out_ref, all_ref = refs[-2:]
    solve(refs[:-2], all_ref)
    rows = out_ref.shape[0]
    upper = lax.axis_index("user") // (lax.axis_size("user") // 2)
    out_ref[...] = all_ref[pl.ds(pl.multiple_of(upper * rows, rows), rows), :]


VMEM = pltpu.VMEM
SMEM = pltpu.SMEM


def call(kernel, outs, *operands, scalars=0, flops=0, scratch=(), limit=16):
    size = sum(op.size * op.dtype.itemsize for op in operands)
    size += sum(4 * math.prod(out.shape) for out in outs)
    spaces = [SMEM] * scalars + [VMEM] * (len(operands) - scalars)
    return pl.pallas_call(
        kernel,
        out_shape=tuple(outs),
        in_specs=[pl.BlockSpec(memory_space=space) for space in spaces],
        out_specs=tuple(pl.BlockSpec(memory_space=VMEM) for unused in outs),
        scratch_shapes=scratch,
        compiler_params=pltpu.CompilerParams(vmem_limit_bytes=limit * MIB),
        cost_estimate=pl.CostEstimate(flops=flops, bytes_accessed=size, transcendentals=0),
    )(*operands)


def shaped(shape, dtype=f32):
    return jax.ShapeDtypeStruct(shape, dtype)


def dense_shards(item_init, tile_rows, tile_cols, tile_count, conf):
    slot_total = tile_rows.shape[-1]
    block, rank = conf.shape[-1], item_init.shape[1]
    half = block // 2
    n_item, n_user = lax.axis_size("item"), lax.axis_size("user")
    row_blocks = UB * n_item
    rows = row_blocks * half
    slots = -(-slot_total // n_user)
    width = 2 * rank
    def swap(value, axis, mask):
        size = n_item if axis == "item" else n_user
        return lax.ppermute(value, axis, [(place, place ^ mask) for place in range(size)])

    def others(value):
        total = value
        mask = 2
        while mask < n_item:
            moved = swap(total, "item", mask)
            if mask * 2 >= n_item:
                return total, moved
            total = total + moved
            mask *= 2

    conf = conf.reshape(slot_total, block, block)
    ids = jnp.concatenate(
        [tile_rows.reshape(-1), tile_cols.reshape(-1), tile_count.reshape(-1)]
    ).astype(jnp.int32)

    def after(value, *tokens):
        return lax.optimization_barrier((value, *tokens))[0]

    named = jnp.concatenate([tile_rows.reshape(1, -1), tile_cols.reshape(1, -1)])
    named = jnp.pad(named.astype(f32), ((0, 6), (0, rank - slot_total)))
    sent = jnp.concatenate([item_init, named], axis=0)
    near = n_user // 2
    token = shaped((8, rank))
    with jax.named_scope("gather_items"):
        pieces = {0: sent}
        for mask in (6, 4, 2, 1):
            pieces[mask] = swap(sent, "user", mask)

    with jax.named_scope("pack_tiles"):
        given, packed = call(
            functools.partial(pack_kernel, slots),
            (
                shaped((slot_total, half, block), jnp.int32),
                pltpu.HBM((near, 2 * slots, block, block), jnp.int32),
            ),
            after(ids, *pieces.values()), conf, scalars=1, flops=10 ** 9,
        )
        other_ids = swap(ids, "item", 1)
        other_half = swap(given, "item", 1)

    with jax.named_scope("gather_items"):
        for mask in (2, 6, 4):
            pieces[mask + 1] = swap(pieces[mask], "user", 1)
        own_items = [pieces[mask] for mask in range(n_user)]
        ids, *own_items, other_half = lax.optimization_barrier((ids, *own_items, other_half))

    with jax.named_scope("send_tiles"):
        halves = [list(range(start, start + near)) for start in (0, near)]
        tiles = lax.all_to_all(
            after(packed, own_items[-1]), "user", 0, 0, tiled=True, axis_index_groups=halves
        )

    with jax.named_scope("gather_items"):
        other_items = [swap(piece, "item", 1) for piece in own_items]

    with jax.named_scope("user_tiles"):
        columns = 2 * n_user * block
        user_conf, user_weight = call(
            functools.partial(user_tiles_kernel, unobserved / (item_init.shape[0] * n_user * n_item)),
            (shaped((rows, columns)), shaped((rows, columns), bf16)),
            ids, other_ids, conf, other_half, scalars=2, flops=10 ** 9,
        )

    def iterate(sides, confidence, pairs, both):
        work = 2 * sides[0].shape[0] * pairs.shape[0] * rank
        states = []
        for place, part in enumerate(sides):
            size = part.shape[0]
            state, begin = shaped(part.shape), place * size
            side, part = call(
                functools.partial(first_kernel, width, begin), (state, state),
                *both(part), confidence, pairs, flops=6 * work,
            )
            states.append((begin, state, (side,), part))
        for kernel in (second_kernel, third_kernel):
            for place, (begin, state, carried, part) in enumerate(states):
                last = shaped((8, state.shape[0])) if kernel is third_kernel else state
                *carried, part = call(
                    functools.partial(kernel, width, begin), (state, state, state, last),
                    *carried, *both(part), confidence, pairs, flops=6 * work,
                )
                states[place] = (begin, state, carried, part)
        return [value for _, _, carried, sums in states for value in (*carried, *both(sums))]

    state = shaped((rows, rank))
    with jax.named_scope("user_cg"):
        *sides, pairs = call(
            functools.partial(user_side_kernel, 2 * n_user),
            (shaped((rows // CHUNKS, rank)),) * CHUNKS + (shaped((columns, 2 * rank), bf16),),
            *own_items, *other_items, user_weight, flops=4 * rows * columns * rank,
        )
        shard = shaped((UB * half, rank))
        users, keep, give = call(
            user_last_kernel, (state, shard, shard),
            *iterate(sides, user_conf, pairs, others), flops=10 ** 6,
        )
        taken = swap(give, "item", 1)
        (user_factors,) = call(
            functools.partial(join_kernel, block), (shaped((UB * block, rank)),), keep, taken
        )

    with jax.named_scope("gather_users"):
        users, tiles = lax.optimization_barrier((users, tiles))
        found = [users, swap(users, "user", 1), swap(users, "user", 2)]

    with jax.named_scope("item_tiles"):
        lists = jnp.stack([pieces[mask][block : block + 2] for mask in range(near)]).astype(jnp.int32)
        columns = near * row_blocks * block
        item_conf, item_weight, laid = call(
            functools.partial(
                item_tiles_kernel, unobserved / (user_factors.shape[0] * n_user * n_item), row_blocks
            ),
            (shaped((2 * block, columns)), shaped((2 * block, columns), bf16), token),
            lists, tiles, scalars=1, flops=10 ** 9,
        )

    with jax.named_scope("gather_users"):
        found.append(swap(after(found[2], laid), "user", 1))
        marks, ordered = [], []
        for mask, piece in enumerate(found):
            marks += [(mask, True), (mask, False)]
            ordered += [piece, swap(piece, "item", 1)]

    def both(value):
        return value, swap(value, "user", near)

    rows = 2 * block
    with jax.named_scope("item_cg"):
        *sides, pairs = call(
            functools.partial(item_side_kernel, row_blocks, block, marks),
            (shaped((rows // CHUNKS, rank)),) * CHUNKS + (shaped((columns, 2 * rank), bf16),),
            *ordered, item_weight, flops=4 * rows * columns * rank,
        )
        item_factors, unused = call(
            item_last_kernel, (shaped((block, rank)), shaped((rows, rank))),
            *iterate(sides, item_conf, pairs, both), flops=10 ** 6,
        )
    return (user_factors, item_factors)


def fits_dense(mesh):
    n_user, n_item = mesh.shape["user"], mesh.shape["item"]
    block = 128
    user_bytes = UB * n_item * block * n_user * block * 4
    return user_bytes <= DENSE_LIMIT and n_item % 2 == 0 and n_user == 8


def block_sum(slot_terms, block_ids, row_count, block_size):
    block_count = row_count // block_size
    targets = jnp.arange(block_count, dtype=jnp.int32)
    onehot = (block_ids[:, None] == targets[None, :]).astype(jnp.float32)
    summed = jnp.einsum("tr,tik->rik", onehot, slot_terms, precision=highest)
    return summed.reshape(row_count, slot_terms.shape[2])


def group_products(own_blocks, other_blocks, tile_values, own_ids, other_ids):
    own_rows = jnp.take(own_blocks, own_ids, axis=0)
    other_rows = jnp.take(other_blocks, other_ids, axis=0)
    scores = jnp.einsum("tik,tjk->tij", own_rows, other_rows, precision=highest)
    return jnp.einsum("tij,tjk->tik", scores * tile_values, other_rows, precision=highest)


def slot_products(own_blocks, other_blocks, tile_values, own_ids, other_ids):
    return group_products(own_blocks, other_blocks, tile_values, own_ids, other_ids)


def conjugate(right_side, apply_operator):
    solution = jnp.zeros_like(right_side)
    residual = right_side
    direction = right_side
    norm_now = jnp.sum(residual * residual, axis=-1, keepdims=True)
    for iteration in range(CG_ITERS):
        product_vec = apply_operator(direction)
        step_length = norm_now / jnp.sum(direction * product_vec, axis=-1, keepdims=True)
        solution = solution + step_length * direction
        residual = residual - step_length * product_vec
        norm_next = jnp.sum(residual * residual, axis=-1, keepdims=True)
        direction = residual + norm_next / norm_now * direction
        norm_now = norm_next
    return solution


def shards(item_init, tile_rows, tile_cols, tile_count, conf):
    slot_total = tile_rows.shape[-1]
    block_size = conf.shape[-1]
    factor_rank = item_init.shape[1]
    item_devices = lax.axis_size("item")
    user_devices = lax.axis_size("user")
    row_ids = tile_rows.reshape(slot_total)
    col_ids = tile_cols.reshape(slot_total)
    slot_count = tile_count.reshape(())
    counts = conf.reshape(slot_total, block_size, block_size).astype(jnp.float32)
    usable = (jnp.arange(slot_total, dtype=jnp.int32) < slot_count)[:, None, None]
    confidence = jnp.where(usable, counts, 0.0)
    weights = jnp.where(usable & (counts > 0.0), 1.0 + counts, 0.0)
    user_rows = UB * block_size
    item_rows = IB * block_size
    item_shard = lax.all_gather(item_init, "user", axis=0, tiled=True)
    item_blocks = item_shard.reshape(-1, block_size, factor_rank)
    item_gram = lax.psum(jnp.dot(item_init.T, item_init, precision=highest), ("user", "item"))
    user_weight = unobserved / (item_init.shape[0] * user_devices * item_devices)
    user_terms = jnp.einsum(
        "tij,tjk->tik", weights, jnp.take(item_blocks, col_ids, axis=0), precision=highest
    )
    user_side = lax.psum_scatter(
        block_sum(user_terms, row_ids, user_rows * lax.axis_size("item"), block_size),
        "item",
        scatter_dimension=0,
        tiled=True,
    )

    def user_operator(direction):
        shard_direction = lax.all_gather(direction, "item", axis=0, tiled=True)
        slot_terms = slot_products(
            shard_direction.reshape(-1, block_size, factor_rank),
            item_blocks,
            confidence,
            row_ids,
            col_ids,
        )
        summed = lax.psum_scatter(
            block_sum(slot_terms, row_ids, user_rows * lax.axis_size("item"), block_size),
            "item",
            scatter_dimension=0,
            tiled=True,
        )
        return (
            summed
            + user_weight * jnp.dot(direction, item_gram, precision=highest)
            + ridge * direction
        )

    user_factors = conjugate(user_side, user_operator)
    user_shard = lax.all_gather(user_factors, "item", axis=0, tiled=True)
    user_blocks = user_shard.reshape(-1, block_size, factor_rank)
    user_gram = lax.psum(jnp.dot(user_factors.T, user_factors, precision=highest), ("user", "item"))
    item_weight = unobserved / (user_factors.shape[0] * user_devices * item_devices)
    confidence_cols = jnp.swapaxes(confidence, 1, 2)
    slot_users = jnp.take(user_blocks, row_ids, axis=0)
    item_terms = jnp.einsum("tij,tik->tjk", weights, slot_users, precision=highest)
    item_side = lax.psum_scatter(
        block_sum(item_terms, col_ids, item_rows * lax.axis_size("user"), block_size),
        "user",
        scatter_dimension=0,
        tiled=True,
    )

    def item_operator(direction):
        shard_direction = lax.all_gather(direction, "user", axis=0, tiled=True)
        slot_terms = slot_products(
            shard_direction.reshape(-1, block_size, factor_rank),
            user_blocks,
            confidence_cols,
            col_ids,
            row_ids,
        )
        summed = lax.psum_scatter(
            block_sum(slot_terms, col_ids, item_rows * lax.axis_size("user"), block_size),
            "user",
            scatter_dimension=0,
            tiled=True,
        )
        return (
            summed
            + item_weight * jnp.dot(direction, user_gram, precision=highest)
            + ridge * direction
        )

    item_factors = conjugate(item_side, item_operator)
    return (user_factors, item_factors)


def solution(mesh):
    in_specs = (
        P(("item", "user"), None),
        P("user", "item", None),
        P("user", "item", None),
        P("user", "item"),
        P("user", "item", None, None, None),
    )
    out_specs = (P(("user", "item"), None), P(("item", "user"), None))
    program = dense_shards if fits_dense(mesh) else shards
    return jax.shard_map(program, mesh=mesh, in_specs=in_specs, out_specs=out_specs, check_vma=False)
```

```python
import functools
import math

import jax
import jax.numpy as jnp
from jax import lax
from jax.experimental import pallas as pl
from jax.experimental.pallas import tpu as pltpu
from jax.sharding import PartitionSpec as P

UB = 2
IB = 1
CG_ITERS = 3
CHUNKS = 2


highest = lax.Precision.HIGHEST
ridge = 5.0
unobserved = 256.0

f32 = jnp.float32
bf16 = jnp.bfloat16
MIB = 1 << 20
DENSE_LIMIT = 8 * MIB


def pair(value):
    high = value.astype(bf16)
    low = (value - high.astype(f32)).astype(bf16)
    return high, low


def row_sum(value):
    return jnp.sum(value, axis=-1, keepdims=True)


def split_rows(value):
    high, low = pair(value)
    return jnp.concatenate(
        [jnp.concatenate([high, low], axis=1), jnp.concatenate([low, high], axis=1)], axis=0
    )


def scores_of(lhs, factors):
    rows = lhs.shape[0] // 2
    both = lax.dot_general(lhs, factors, (((1,), (1,)), ((), ())), preferred_element_type=f32)
    return both[:rows] + both[rows:]


def tile_terms(direction, conf_ref, pairs_ref, width, begin):
    rows, rank = direction.shape
    lhs = split_rows(direction)
    total = jnp.zeros((rows, rank), f32)
    for start in range(0, conf_ref.shape[1], width):
        factors = pairs_ref[start : start + width, :]
        weighted = scores_of(lhs, factors) * conf_ref[begin : begin + rows, start : start + width]
        high, low = pair(weighted)
        out = jnp.dot(jnp.concatenate([high, low], axis=0), factors, preferred_element_type=f32)
        total = total + (
            (out[:rows, :rank] + out[:rows, rank:]) + (out[rows:, :rank] + out[rows:, rank:])
        )
    return total


def tile_squares(direction, conf_ref, pairs_ref, width, begin):
    rows, rank = direction.shape
    lhs = split_rows(direction)
    total = jnp.zeros((rows, rank), f32)
    for start in range(0, conf_ref.shape[1], width):
        scores = scores_of(lhs, pairs_ref[start : start + width, :])
        squares = scores * scores * conf_ref[begin : begin + rows, start : start + width]
        for part in range(0, width, rank):
            total = total + squares[:, part : part + rank]
    return total


def write_sides(weight_ref, pairs_ref, side_refs):
    rank = pairs_ref.shape[1] // 2
    both = jnp.dot(weight_ref[...], pairs_ref[...], preferred_element_type=f32)
    start = 0
    for side_ref in side_refs:
        rows = slice(start, start + side_ref.shape[0])
        side_ref[...] = both[rows, :rank] + both[rows, rank:]
        start += side_ref.shape[0]


def advance(solution, residual, direction, product):
    norm_now = row_sum(residual * residual)
    step_length = norm_now / row_sum(direction * product)
    solution = solution + step_length * direction
    residual = residual - step_length * product
    direction = residual + row_sum(residual * residual) / norm_now * direction
    return solution, residual, direction


def pack_kernel(slots, ids_ref, conf_ref, given_ref, send_ref):
    slot_total, block, _ = conf_ref.shape
    half = block // 2
    owners = slot_total // slots
    near = owners // 2
    core = lax.rem(lax.axis_index("item"), 2)
    shift = ids_ref[slot_total]
    count = ids_ref[2 * slot_total]
    given_ref[...] = conf_ref[:, pl.ds(pl.multiple_of((1 - core) * half, half), half), :]
    for owner in range(owners):
        first = lax.rem(owner - shift + owners, owners)
        for slot in range(slots):
            place = first + owners * slot
            used = place < jnp.minimum(count, slot_total)
            send_ref[owner % near, owner // near * slots + slot] = jnp.where(used, conf_ref[place], 0)


def user_tiles_kernel(weight_zero, own_ids, other_ids, conf_ref, half_ref, dense_ref, weight_ref):
    slot_total, block, _ = conf_ref.shape
    half = block // 2
    owners = dense_ref.shape[1] // block // 2
    me = lax.axis_index("user")
    core = lax.rem(lax.axis_index("item"), 2)
    dense_ref[...] = jnp.full(dense_ref.shape, weight_zero, f32)
    weight_ref[...] = jnp.zeros(weight_ref.shape, bf16)

    def place(ids, slot, base, counts):
        row = pl.multiple_of(ids[slot] * half, half)
        col = pl.multiple_of((base + jnp.bitwise_xor(ids[slot_total + slot], me)) * block, block)
        at = (pl.ds(row, half), pl.ds(col, block))
        value = counts.astype(f32)
        dense_ref[at] = dense_ref[at] + value
        weight_ref[at] = weight_ref[at] + jnp.where(value > 0.0, 1.0 + value, 0.0).astype(bf16)

    def own(slot, carry):
        rows = pl.ds(pl.multiple_of(core * half, half), half)
        place(own_ids, slot, 0, conf_ref[slot, rows, :])
        return carry

    def other(slot, carry):
        place(other_ids, slot, owners, half_ref[slot])
        return carry

    lax.fori_loop(0, jnp.minimum(own_ids[2 * slot_total], slot_total), own, 0)
    lax.fori_loop(0, jnp.minimum(other_ids[2 * slot_total], slot_total), other, 0)


def user_side_kernel(count, *refs):
    pieces, (weight_ref, *side_refs, pairs_ref) = refs[:count], refs[count:]
    block = pairs_ref.shape[0] // count
    for place, piece in enumerate(pieces):
        high, low = pair(piece[:block, :])
        pairs_ref[place * block : (place + 1) * block, :] = jnp.concatenate([high, low], axis=1)
    write_sides(weight_ref, pairs_ref, side_refs)


def first_kernel(width, begin, own_ref, other_ref, conf_ref, pairs_ref, side_ref, out_ref):
    side = own_ref[...] + other_ref[...]
    side_ref[...] = side
    out_ref[...] = tile_terms(side, conf_ref, pairs_ref, width, begin)


def second_kernel(
    width, begin, side_ref, own_ref, other_ref, conf_ref, pairs_ref, x_ref, r_ref, d_ref, out_ref
):
    side = side_ref[...]
    product = own_ref[...] + other_ref[...] + ridge * side
    x, r, d = advance(jnp.zeros_like(side), side, side, product)
    x_ref[...] = x
    r_ref[...] = r
    d_ref[...] = d
    out_ref[...] = tile_terms(d, conf_ref, pairs_ref, width, begin)


def third_kernel(
    width, begin, x_in, r_in, d_in, own_ref, other_ref, conf_ref, pairs_ref, x_ref, r_ref, d_ref, sums_ref
):
    direction = d_in[...]
    product = own_ref[...] + other_ref[...] + ridge * direction
    x, r, d = advance(x_in[...], r_in[...], direction, product)
    x_ref[...] = x
    r_ref[...] = r
    d_ref[...] = d
    squares = tile_squares(d, conf_ref, pairs_ref, width, begin)
    ones = jnp.ones((8, squares.shape[1]), bf16)
    sums = jnp.zeros(sums_ref.shape, f32)
    for unused in range(3):
        part = squares.astype(bf16)
        squares = squares - part.astype(f32)
        sums = sums + lax.dot_general(ones, part, (((1,), (1,)), ((), ())), preferred_element_type=f32)
    sums_ref[...] = sums


def solve(refs, out_ref):
    start = 0
    for place in range(0, len(refs), 5):
        x_in, r_in, d_in, own_ref, other_ref = refs[place : place + 5]
        residual, direction = r_in[...], d_in[...]
        sums = jnp.transpose(own_ref[...] + other_ref[...])[:, :1]
        length = row_sum(residual * residual) / (sums + ridge * row_sum(direction * direction))
        out_ref[start : start + residual.shape[0], :] = x_in[...] + length * direction
        start += residual.shape[0]


def user_last_kernel(*refs):
    out_ref, keep_ref, give_ref = refs[-3:]
    solve(refs[:-3], out_ref)
    place = lax.axis_index("item")
    rows = keep_ref.shape[0]
    keep_ref[...] = out_ref[pl.ds(pl.multiple_of(place * rows, rows), rows), :]
    other = jnp.bitwise_xor(place, 1)
    give_ref[...] = out_ref[pl.ds(pl.multiple_of(other * rows, rows), rows), :]


def item_tiles_kernel(weight_zero, row_blocks, lists_ref, tiles_ref, dense_ref, weight_ref):
    near, count, block, _ = tiles_ref.shape
    slots = count // 2
    me = lax.rem(lax.axis_index("user"), near)
    dense_ref[...] = jnp.full(dense_ref.shape, weight_zero, f32)
    weight_ref[...] = jnp.zeros(weight_ref.shape, bf16)
    for source in range(near):
        mask = jnp.bitwise_xor(source, me)
        for upper in range(2):
            first = lax.rem(me + upper * near - lists_ref[mask, 1, 0] + 2 * near, 2 * near)
            for slot in range(slots):
                value = jnp.transpose(tiles_ref[source, upper * slots + slot].astype(f32))
                row = lists_ref[mask, 0, first + 2 * near * slot]
                col = pl.multiple_of((mask * row_blocks + row) * block, block)
                at = (slice(upper * block, (upper + 1) * block), pl.ds(col, block))
                dense_ref[at] = dense_ref[at] + value
                weight_ref[at] = weight_ref[at] + jnp.where(value > 0.0, 1.0 + value, 0.0).astype(bf16)


def join_kernel(block, own_ref, other_ref, out_ref):
    half = block // 2
    core = lax.rem(lax.axis_index("item"), 2)
    for start in range(0, out_ref.shape[0], block):
        for offset, part_ref in ((core, own_ref), (1 - core, other_ref)):
            rows = pl.ds(pl.multiple_of(start + offset * half, half), half)
            out_ref[rows, :] = part_ref[start // 2 : start // 2 + half, :]


def item_side_kernel(row_blocks, block, marks, *refs):
    pieces, (weight_ref, *side_refs, pairs_ref) = refs[: len(marks)], refs[len(marks) :]
    half = block // 2
    core = lax.rem(lax.axis_index("item"), 2)
    for (mask, own_half), piece in zip(marks, pieces):
        offset = pl.multiple_of((core if own_half else 1 - core) * half, half)
        for row in range(row_blocks):
            high, low = pair(piece[row * half : (row + 1) * half, :])
            start = (mask * row_blocks + row) * block
            pairs_ref[pl.ds(start + offset, half), :] = jnp.concatenate([high, low], axis=1)
    write_sides(weight_ref, pairs_ref, side_refs)


def item_last_kernel(*refs):
    out_ref, all_ref = refs[-2:]
    solve(refs[:-2], all_ref)
    rows = out_ref.shape[0]
    upper = lax.axis_index("user") // (lax.axis_size("user") // 2)
    out_ref[...] = all_ref[pl.ds(pl.multiple_of(upper * rows, rows), rows), :]


VMEM = pltpu.VMEM
SMEM = pltpu.SMEM


def call(kernel, outs, *operands, scalars=0, flops=0, scratch=(), limit=16):
    size = sum(op.size * op.dtype.itemsize for op in operands)
    size += sum(4 * math.prod(out.shape) for out in outs)
    spaces = [SMEM] * scalars + [VMEM] * (len(operands) - scalars)
    return pl.pallas_call(
        kernel,
        out_shape=tuple(outs),
        in_specs=[pl.BlockSpec(memory_space=space) for space in spaces],
        out_specs=tuple(pl.BlockSpec(memory_space=VMEM) for unused in outs),
        scratch_shapes=scratch,
        compiler_params=pltpu.CompilerParams(vmem_limit_bytes=limit * MIB),
        cost_estimate=pl.CostEstimate(flops=flops, bytes_accessed=size, transcendentals=0),
    )(*operands)


def shaped(shape, dtype=f32):
    return jax.ShapeDtypeStruct(shape, dtype)


def dense_shards(item_init, tile_rows, tile_cols, tile_count, conf):
    slot_total = tile_rows.shape[-1]
    block, rank = conf.shape[-1], item_init.shape[1]
    half = block // 2
    n_item, n_user = lax.axis_size("item"), lax.axis_size("user")
    row_blocks = UB * n_item
    rows = row_blocks * half
    slots = -(-slot_total // n_user)
    width = 2 * rank
    def swap(value, axis, mask):
        size = n_item if axis == "item" else n_user
        return lax.ppermute(value, axis, [(place, place ^ mask) for place in range(size)])

    def others(value):
        total = value
        mask = 2
        while mask < n_item:
            moved = swap(total, "item", mask)
            if mask * 2 >= n_item:
                return total, moved
            total = total + moved
            mask *= 2

    conf = conf.reshape(slot_total, block, block)
    ids = jnp.concatenate(
        [tile_rows.reshape(-1), tile_cols.reshape(-1), tile_count.reshape(-1)]
    ).astype(jnp.int32)

    def after(value, *tokens):
        return lax.optimization_barrier((value, *tokens))[0]

    named = jnp.concatenate([tile_rows.reshape(1, -1), tile_cols.reshape(1, -1)])
    named = jnp.pad(named.astype(f32), ((0, 6), (0, rank - slot_total)))
    sent = jnp.concatenate([item_init, named], axis=0)
    near = n_user // 2
    with jax.named_scope("gather_items"):
        pieces = {0: sent}
        for mask in (6, 4, 2, 1):
            pieces[mask] = swap(sent, "user", mask)

    with jax.named_scope("gather_items"):
        for mask in (2, 6, 4):
            pieces[mask + 1] = swap(pieces[mask], "user", 1)
        own_items = [pieces[mask] for mask in range(n_user)]
        other_items = [swap(piece, "item", 1) for piece in own_items]

    with jax.named_scope("pack_tiles"):
        given, packed = call(
            functools.partial(pack_kernel, slots),
            (
                pltpu.HBM((slot_total, half, block), jnp.int32),
                pltpu.HBM((near, 2 * slots, block, block), jnp.int32),
            ),
            after(ids, pieces[3]), conf, scalars=1, flops=10 ** 9,
        )
        other_ids = swap(ids, "item", 1)
        other_half = swap(given, "item", 1)

    with jax.named_scope("send_tiles"):
        halves = [list(range(start, start + near)) for start in (0, near)]
        tiles = lax.all_to_all(
            after(packed, *own_items), "user", 0, 0, tiled=True, axis_index_groups=halves
        )
        ids = after(ids, *own_items)

    with jax.named_scope("user_tiles"):
        columns = 2 * n_user * block
        user_conf, user_weight = call(
            functools.partial(user_tiles_kernel, unobserved / (item_init.shape[0] * n_user * n_item)),
            (shaped((rows, columns)), shaped((rows, columns), bf16)),
            ids, other_ids, conf, other_half, scalars=2, flops=10 ** 9,
        )

    def iterate(sides, confidence, pairs, both):
        work = 2 * sides[0].shape[0] * pairs.shape[0] * rank
        states = []
        for place, part in enumerate(sides):
            size = part.shape[0]
            state, begin = shaped(part.shape), place * size
            side, part = call(
                functools.partial(first_kernel, width, begin), (state, state),
                *both(part), confidence, pairs, flops=6 * work,
            )
            states.append((begin, state, (side,), part))
        for kernel in (second_kernel, third_kernel):
            for place, (begin, state, carried, part) in enumerate(states):
                last = shaped((8, state.shape[0])) if kernel is third_kernel else state
                *carried, part = call(
                    functools.partial(kernel, width, begin), (state, state, state, last),
                    *carried, *both(part), confidence, pairs, flops=6 * work,
                )
                states[place] = (begin, state, carried, part)
        return [value for _, _, carried, sums in states for value in (*carried, *both(sums))]

    state = shaped((rows, rank))
    with jax.named_scope("user_cg"):
        *sides, pairs = call(
            functools.partial(user_side_kernel, 2 * n_user),
            (shaped((rows // CHUNKS, rank)),) * CHUNKS + (shaped((columns, 2 * rank), bf16),),
            *own_items, *other_items, user_weight, flops=4 * rows * columns * rank,
        )
        shard = shaped((UB * half, rank))
        users, keep, give = call(
            user_last_kernel, (state, shard, shard),
            *iterate(sides, user_conf, pairs, others), flops=10 ** 6,
        )
        taken = swap(give, "item", 1)
        (user_factors,) = call(
            functools.partial(join_kernel, block), (shaped((UB * block, rank)),), keep, taken
        )

    with jax.named_scope("gather_users"):
        users, tiles = lax.optimization_barrier((users, tiles))
        found = [users, swap(users, "user", 1), swap(users, "user", 2)]

    with jax.named_scope("item_tiles"):
        lists = jnp.stack([pieces[mask][block : block + 2] for mask in range(near)]).astype(jnp.int32)
        columns = near * row_blocks * block
        item_conf, item_weight = call(
            functools.partial(
                item_tiles_kernel, unobserved / (user_factors.shape[0] * n_user * n_item), row_blocks
            ),
            (shaped((2 * block, columns)), shaped((2 * block, columns), bf16)),
            lists, tiles, scalars=1, flops=10 ** 9,
        )

    with jax.named_scope("gather_users"):
        neighbour, item_conf = lax.optimization_barrier((found[2], item_conf))
        found.append(swap(neighbour, "user", 1))
        marks, ordered = [], []
        for mask, piece in enumerate(found):
            marks += [(mask, True), (mask, False)]
            ordered += [piece, swap(piece, "item", 1)]

    def both(value):
        return value, swap(value, "user", near)

    rows = 2 * block
    with jax.named_scope("item_cg"):
        *sides, pairs = call(
            functools.partial(item_side_kernel, row_blocks, block, marks),
            (shaped((rows // CHUNKS, rank)),) * CHUNKS + (shaped((columns, 2 * rank), bf16),),
            *ordered, item_weight, flops=4 * rows * columns * rank,
        )
        item_factors, unused = call(
            item_last_kernel, (shaped((block, rank)), shaped((rows, rank))),
            *iterate(sides, item_conf, pairs, both), flops=10 ** 6,
        )
    return (user_factors, item_factors)


def fits_dense(mesh):
    n_user, n_item = mesh.shape["user"], mesh.shape["item"]
    block = 128
    user_bytes = UB * n_item * block * n_user * block * 4
    return user_bytes <= DENSE_LIMIT and n_item % 2 == 0 and n_user == 8


def block_sum(slot_terms, block_ids, row_count, block_size):
    block_count = row_count // block_size
    targets = jnp.arange(block_count, dtype=jnp.int32)
    onehot = (block_ids[:, None] == targets[None, :]).astype(jnp.float32)
    summed = jnp.einsum("tr,tik->rik", onehot, slot_terms, precision=highest)
    return summed.reshape(row_count, slot_terms.shape[2])


def group_products(own_blocks, other_blocks, tile_values, own_ids, other_ids):
    own_rows = jnp.take(own_blocks, own_ids, axis=0)
    other_rows = jnp.take(other_blocks, other_ids, axis=0)
    scores = jnp.einsum("tik,tjk->tij", own_rows, other_rows, precision=highest)
    return jnp.einsum("tij,tjk->tik", scores * tile_values, other_rows, precision=highest)


def slot_products(own_blocks, other_blocks, tile_values, own_ids, other_ids):
    return group_products(own_blocks, other_blocks, tile_values, own_ids, other_ids)


def conjugate(right_side, apply_operator):
    solution = jnp.zeros_like(right_side)
    residual = right_side
    direction = right_side
    norm_now = jnp.sum(residual * residual, axis=-1, keepdims=True)
    for iteration in range(CG_ITERS):
        product_vec = apply_operator(direction)
        step_length = norm_now / jnp.sum(direction * product_vec, axis=-1, keepdims=True)
        solution = solution + step_length * direction
        residual = residual - step_length * product_vec
        norm_next = jnp.sum(residual * residual, axis=-1, keepdims=True)
        direction = residual + norm_next / norm_now * direction
        norm_now = norm_next
    return solution


def shards(item_init, tile_rows, tile_cols, tile_count, conf):
    slot_total = tile_rows.shape[-1]
    block_size = conf.shape[-1]
    factor_rank = item_init.shape[1]
    item_devices = lax.axis_size("item")
    user_devices = lax.axis_size("user")
    row_ids = tile_rows.reshape(slot_total)
    col_ids = tile_cols.reshape(slot_total)
    slot_count = tile_count.reshape(())
    counts = conf.reshape(slot_total, block_size, block_size).astype(jnp.float32)
    usable = (jnp.arange(slot_total, dtype=jnp.int32) < slot_count)[:, None, None]
    confidence = jnp.where(usable, counts, 0.0)
    weights = jnp.where(usable & (counts > 0.0), 1.0 + counts, 0.0)
    user_rows = UB * block_size
    item_rows = IB * block_size
    item_shard = lax.all_gather(item_init, "user", axis=0, tiled=True)
    item_blocks = item_shard.reshape(-1, block_size, factor_rank)
    item_gram = lax.psum(jnp.dot(item_init.T, item_init, precision=highest), ("user", "item"))
    user_weight = unobserved / (item_init.shape[0] * user_devices * item_devices)
    user_terms = jnp.einsum(
        "tij,tjk->tik", weights, jnp.take(item_blocks, col_ids, axis=0), precision=highest
    )
    user_side = lax.psum_scatter(
        block_sum(user_terms, row_ids, user_rows * lax.axis_size("item"), block_size),
        "item",
        scatter_dimension=0,
        tiled=True,
    )

    def user_operator(direction):
        shard_direction = lax.all_gather(direction, "item", axis=0, tiled=True)
        slot_terms = slot_products(
            shard_direction.reshape(-1, block_size, factor_rank),
            item_blocks,
            confidence,
            row_ids,
            col_ids,
        )
        summed = lax.psum_scatter(
            block_sum(slot_terms, row_ids, user_rows * lax.axis_size("item"), block_size),
            "item",
            scatter_dimension=0,
            tiled=True,
        )
        return (
            summed
            + user_weight * jnp.dot(direction, item_gram, precision=highest)
            + ridge * direction
        )

    user_factors = conjugate(user_side, user_operator)
    user_shard = lax.all_gather(user_factors, "item", axis=0, tiled=True)
    user_blocks = user_shard.reshape(-1, block_size, factor_rank)
    user_gram = lax.psum(jnp.dot(user_factors.T, user_factors, precision=highest), ("user", "item"))
    item_weight = unobserved / (user_factors.shape[0] * user_devices * item_devices)
    confidence_cols = jnp.swapaxes(confidence, 1, 2)
    slot_users = jnp.take(user_blocks, row_ids, axis=0)
    item_terms = jnp.einsum("tij,tik->tjk", weights, slot_users, precision=highest)
    item_side = lax.psum_scatter(
        block_sum(item_terms, col_ids, item_rows * lax.axis_size("user"), block_size),
        "user",
        scatter_dimension=0,
        tiled=True,
    )

    def item_operator(direction):
        shard_direction = lax.all_gather(direction, "user", axis=0, tiled=True)
        slot_terms = slot_products(
            shard_direction.reshape(-1, block_size, factor_rank),
            user_blocks,
            confidence_cols,
            col_ids,
            row_ids,
        )
        summed = lax.psum_scatter(
            block_sum(slot_terms, col_ids, item_rows * lax.axis_size("user"), block_size),
            "user",
            scatter_dimension=0,
            tiled=True,
        )
        return (
            summed
            + item_weight * jnp.dot(direction, user_gram, precision=highest)
            + ridge * direction
        )

    item_factors = conjugate(item_side, item_operator)
    return (user_factors, item_factors)


def solution(mesh):
    in_specs = (
        P(("item", "user"), None),
        P("user", "item", None),
        P("user", "item", None),
        P("user", "item"),
        P("user", "item", None, None, None),
    )
    out_specs = (P(("user", "item"), None), P(("item", "user"), None))
    program = dense_shards if fits_dense(mesh) else shards
    return jax.shard_map(program, mesh=mesh, in_specs=in_specs, out_specs=out_specs, check_vma=False)
```

```python
import functools
import math

import jax
import jax.numpy as jnp
from jax import lax
from jax.experimental import pallas as pl
from jax.experimental.pallas import tpu as pltpu
from jax.sharding import PartitionSpec as P

UB = 2
IB = 1
CG_ITERS = 3
CHUNKS = 2


highest = lax.Precision.HIGHEST
ridge = 5.0
unobserved = 256.0

f32 = jnp.float32
bf16 = jnp.bfloat16
MIB = 1 << 20
DENSE_LIMIT = 8 * MIB


def pair(value):
    high = value.astype(bf16)
    low = (value - high.astype(f32)).astype(bf16)
    return high, low


def row_sum(value):
    return jnp.sum(value, axis=-1, keepdims=True)


def split_rows(value):
    high, low = pair(value)
    return jnp.concatenate(
        [jnp.concatenate([high, low], axis=1), jnp.concatenate([low, high], axis=1)], axis=0
    )


def scores_of(lhs, factors):
    rows = lhs.shape[0] // 2
    both = lax.dot_general(lhs, factors, (((1,), (1,)), ((), ())), preferred_element_type=f32)
    return both[:rows] + both[rows:]


def tile_terms(direction, conf_ref, pairs_ref, width, begin):
    rows, rank = direction.shape
    lhs = split_rows(direction)
    total = jnp.zeros((rows, rank), f32)
    for start in range(0, conf_ref.shape[1], width):
        factors = pairs_ref[start : start + width, :]
        weighted = scores_of(lhs, factors) * conf_ref[begin : begin + rows, start : start + width]
        high, low = pair(weighted)
        out = jnp.dot(jnp.concatenate([high, low], axis=0), factors, preferred_element_type=f32)
        total = total + (
            (out[:rows, :rank] + out[:rows, rank:]) + (out[rows:, :rank] + out[rows:, rank:])
        )
    return total


def tile_squares(direction, conf_ref, pairs_ref, width, begin):
    rows, rank = direction.shape
    lhs = split_rows(direction)
    total = jnp.zeros((rows, rank), f32)
    for start in range(0, conf_ref.shape[1], width):
        scores = scores_of(lhs, pairs_ref[start : start + width, :])
        squares = scores * scores * conf_ref[begin : begin + rows, start : start + width]
        for part in range(0, width, rank):
            total = total + squares[:, part : part + rank]
    return total


def write_sides(weight_ref, pairs_ref, side_refs):
    rank = pairs_ref.shape[1] // 2
    both = jnp.dot(weight_ref[...], pairs_ref[...], preferred_element_type=f32)
    start = 0
    for side_ref in side_refs:
        rows = slice(start, start + side_ref.shape[0])
        side_ref[...] = both[rows, :rank] + both[rows, rank:]
        start += side_ref.shape[0]


def advance(solution, residual, direction, product):
    norm_now = row_sum(residual * residual)
    step_length = norm_now / row_sum(direction * product)
    solution = solution + step_length * direction
    residual = residual - step_length * product
    direction = residual + row_sum(residual * residual) / norm_now * direction
    return solution, residual, direction


def pack_kernel(slots, ids_ref, conf_ref, named_ref, given_ref, send_ref, held, in_sems, sems):
    slot_total, block, _ = conf_ref.shape
    half = block // 2
    owners = slot_total // slots
    near = owners // 2
    core = lax.rem(lax.axis_index("item"), 2)
    taken = [
        pltpu.make_async_copy(conf_ref.at[slot], held.at[slot], in_sems.at[slot]) for slot in range(slot_total)
    ]
    for copy in taken:
        copy.start()
    copies = []
    for owner in range(near):
        target = send_ref.at[owner, 2 * slots * block :, :]
        copies.append(pltpu.make_async_copy(named_ref, target, sems.at[len(copies)]))
        copies[-1].start()
    for slot in range(slot_total):
        owner = lax.rem(ids_ref[1, 0] + slot, owners)
        start = pl.multiple_of((owner // near * slots + slot // owners) * block, block)
        target = send_ref.at[lax.rem(owner, near), pl.ds(start, block), :]
        taken[slot].wait()
        copies.append(pltpu.make_async_copy(held.at[slot], target, sems.at[len(copies)]))
        copies[-1].start()
    rows = pl.ds(pl.multiple_of((1 - core) * half, half), half)
    copies.append(pltpu.make_async_copy(held.at[:, rows, :], given_ref, sems.at[len(copies)]))
    copies[-1].start()
    for copy in copies:
        copy.wait()


def user_tile(named_ref, slot, base, counts, dense_ref, weight_ref):
    half, block = counts.shape
    owners = dense_ref.shape[1] // block // 2
    owner = lax.rem(named_ref[1, 0] + slot, owners)
    row = pl.multiple_of(named_ref[0, slot] * half, half)
    col = pl.multiple_of((base + jnp.bitwise_xor(owner, lax.axis_index("user"))) * block, block)
    at = (pl.ds(row, half), pl.ds(col, block))
    value = counts.astype(f32)
    dense_ref[at] = dense_ref[at] + value
    weight_ref[at] = weight_ref[at] + jnp.where(value > 0.0, 1.0 + value, 0.0).astype(bf16)


def own_tiles_kernel(weight_zero, named_ref, conf_ref, dense_ref, weight_ref, held, sem):
    slot_total, block, _ = conf_ref.shape
    half = block // 2
    core = lax.rem(lax.axis_index("item"), 2)
    rows = pl.ds(pl.multiple_of(core * half, half), half)
    copy = pltpu.make_async_copy(conf_ref.at[:, rows, :], held, sem)
    copy.start()
    dense_ref[...] = jnp.full(dense_ref.shape, weight_zero, f32)
    weight_ref[...] = jnp.zeros(weight_ref.shape, bf16)
    copy.wait()

    def one(slot, carry):
        user_tile(named_ref, slot, 0, held[slot], dense_ref, weight_ref)
        return carry

    lax.fori_loop(0, jnp.minimum(named_ref[1, 1], slot_total), one, 0)


def other_tiles_kernel(named_ref, half_ref, dense_in, weight_in, dense_ref, weight_ref):
    slot_total, _, block = half_ref.shape
    owners = dense_ref.shape[1] // block // 2

    def one(slot, carry):
        user_tile(named_ref, slot, owners, half_ref[slot], dense_ref, weight_ref)
        return carry

    lax.fori_loop(0, jnp.minimum(named_ref[1, 1], slot_total), one, 0)


def user_side_kernel(count, *refs):
    pieces, (weight_ref, *side_refs, pairs_ref) = refs[:count], refs[count:]
    block = pairs_ref.shape[0] // count
    for place, piece in enumerate(pieces):
        high, low = pair(piece[:block, :])
        pairs_ref[place * block : (place + 1) * block, :] = jnp.concatenate([high, low], axis=1)
    write_sides(weight_ref, pairs_ref, side_refs)


def first_kernel(width, begin, own_ref, other_ref, conf_ref, pairs_ref, side_ref, out_ref):
    side = own_ref[...] + other_ref[...]
    side_ref[...] = side
    out_ref[...] = tile_terms(side, conf_ref, pairs_ref, width, begin)


def second_kernel(
    width, begin, side_ref, own_ref, other_ref, conf_ref, pairs_ref, x_ref, r_ref, d_ref, out_ref
):
    side = side_ref[...]
    product = own_ref[...] + other_ref[...] + ridge * side
    x, r, d = advance(jnp.zeros_like(side), side, side, product)
    x_ref[...] = x
    r_ref[...] = r
    d_ref[...] = d
    out_ref[...] = tile_terms(d, conf_ref, pairs_ref, width, begin)


def third_kernel(
    width, begin, x_in, r_in, d_in, own_ref, other_ref, conf_ref, pairs_ref, x_ref, r_ref, d_ref, sums_ref
):
    direction = d_in[...]
    product = own_ref[...] + other_ref[...] + ridge * direction
    x, r, d = advance(x_in[...], r_in[...], direction, product)
    x_ref[...] = x
    r_ref[...] = r
    d_ref[...] = d
    squares = tile_squares(d, conf_ref, pairs_ref, width, begin)
    ones = jnp.ones((8, squares.shape[1]), bf16)
    sums = jnp.zeros(sums_ref.shape, f32)
    for unused in range(3):
        part = squares.astype(bf16)
        squares = squares - part.astype(f32)
        sums = sums + lax.dot_general(ones, part, (((1,), (1,)), ((), ())), preferred_element_type=f32)
    sums_ref[...] = sums


def solve(refs, out_ref):
    start = 0
    for place in range(0, len(refs), 5):
        x_in, r_in, d_in, own_ref, other_ref = refs[place : place + 5]
        residual, direction = r_in[...], d_in[...]
        sums = jnp.transpose(own_ref[...] + other_ref[...])[:, :1]
        length = row_sum(residual * residual) / (sums + ridge * row_sum(direction * direction))
        out_ref[start : start + residual.shape[0], :] = x_in[...] + length * direction
        start += residual.shape[0]


def user_last_kernel(*refs):
    out_ref, keep_ref, give_ref = refs[-3:]
    solve(refs[:-3], out_ref)
    place = lax.axis_index("item")
    rows = keep_ref.shape[0]
    keep_ref[...] = out_ref[pl.ds(pl.multiple_of(place * rows, rows), rows), :]
    other = jnp.bitwise_xor(place, 1)
    give_ref[...] = out_ref[pl.ds(pl.multiple_of(other * rows, rows), rows), :]


def item_tiles_kernel(weight_zero, row_blocks, slots, lists_ref, tiles_ref, dense_ref, weight_ref):
    near = tiles_ref.shape[0]
    block = tiles_ref.shape[2]
    me = lax.rem(lax.axis_index("user"), near)
    dense_ref[...] = jnp.full(dense_ref.shape, weight_zero, f32)
    weight_ref[...] = jnp.zeros(weight_ref.shape, bf16)
    for source in range(near):
        mask = jnp.bitwise_xor(source, me)
        for upper in range(2):
            first = lax.rem(me + upper * near - lists_ref[source, 1, 0] + 2 * near, 2 * near)
            for slot in range(slots):
                start = (upper * slots + slot) * block
                place = first + 2 * near * slot
                used = place < lists_ref[source, 1, 1]
                tile = jnp.where(used, tiles_ref[source, start : start + block, :], 0)
                value = jnp.transpose(tile.astype(f32))
                row = lists_ref[source, 0, place]
                col = pl.multiple_of((mask * row_blocks + row) * block, block)
                at = (slice(upper * block, (upper + 1) * block), pl.ds(col, block))
                dense_ref[at] = dense_ref[at] + value
                weight_ref[at] = weight_ref[at] + jnp.where(value > 0.0, 1.0 + value, 0.0).astype(bf16)


def join_kernel(block, own_ref, other_ref, out_ref):
    half = block // 2
    core = lax.rem(lax.axis_index("item"), 2)
    for start in range(0, out_ref.shape[0], block):
        for offset, part_ref in ((core, own_ref), (1 - core, other_ref)):
            rows = pl.ds(pl.multiple_of(start + offset * half, half), half)
            out_ref[rows, :] = part_ref[start // 2 : start // 2 + half, :]


def item_side_kernel(row_blocks, block, marks, *refs):
    pieces, (weight_ref, *side_refs, pairs_ref) = refs[: len(marks)], refs[len(marks) :]
    half = block // 2
    core = lax.rem(lax.axis_index("item"), 2)
    for (mask, own_half), piece in zip(marks, pieces):
        offset = pl.multiple_of((core if own_half else 1 - core) * half, half)
        for row in range(row_blocks):
            high, low = pair(piece[row * half : (row + 1) * half, :])
            start = (mask * row_blocks + row) * block
            pairs_ref[pl.ds(start + offset, half), :] = jnp.concatenate([high, low], axis=1)
    write_sides(weight_ref, pairs_ref, side_refs)


def item_last_kernel(*refs):
    out_ref, all_ref = refs[-2:]
    solve(refs[:-2], all_ref)
    rows = out_ref.shape[0]
    upper = lax.axis_index("user") // (lax.axis_size("user") // 2)
    out_ref[...] = all_ref[pl.ds(pl.multiple_of(upper * rows, rows), rows), :]


VMEM = pltpu.VMEM
SMEM = pltpu.SMEM


def call(kernel, outs, *operands, scalars=0, far=0, far_outs=0, flops=0, scratch=(), limit=16, aliases=None):
    size = sum(op.size * op.dtype.itemsize for op in operands)
    size += sum(4 * math.prod(out.shape) for out in outs)
    spaces = [SMEM] * scalars + [pl.ANY] * far + [VMEM] * (len(operands) - scalars - far)
    return pl.pallas_call(
        kernel,
        out_shape=tuple(outs),
        in_specs=[pl.BlockSpec(memory_space=space) for space in spaces],
        out_specs=tuple(pl.BlockSpec(memory_space=pl.ANY if place < far_outs else VMEM) for place in range(len(outs))),
        scratch_shapes=scratch,
        input_output_aliases=aliases or {},
        compiler_params=pltpu.CompilerParams(vmem_limit_bytes=limit * MIB),
        cost_estimate=pl.CostEstimate(flops=flops, bytes_accessed=size, transcendentals=0),
    )(*operands)


def shaped(shape, dtype=f32):
    return jax.ShapeDtypeStruct(shape, dtype)


def dense_shards(item_init, tile_rows, tile_cols, tile_count, conf):
    slot_total = tile_rows.shape[-1]
    block, rank = conf.shape[-1], item_init.shape[1]
    half = block // 2
    n_item, n_user = lax.axis_size("item"), lax.axis_size("user")
    row_blocks = UB * n_item
    rows = row_blocks * half
    slots = -(-slot_total // n_user)
    width = 2 * rank
    def swap(value, axis, mask):
        size = n_item if axis == "item" else n_user
        return lax.ppermute(value, axis, [(place, place ^ mask) for place in range(size)])

    def others(value):
        total = value
        mask = 2
        while mask < n_item:
            moved = swap(total, "item", mask)
            if mask * 2 >= n_item:
                return total, moved
            total = total + moved
            mask *= 2

    conf = conf.reshape(slot_total, block, block)
    def after(value, *tokens):
        return lax.optimization_barrier((value, *tokens))[0]

    named = sum(
        jnp.pad(value.reshape(1, -1), ((row, 7 - row), (lane, rank - lane - size)))
        for value, row, lane, size in (
            (tile_rows, 0, 0, slot_total), (tile_cols[..., :1], 1, 0, 1), (tile_count, 1, 1, 1)
        )
    )
    near = n_user // 2
    with jax.named_scope("gather_items"):
        pieces = {0: item_init}
        for mask in (6, 4, 2, 1):
            pieces[mask] = swap(item_init, "user", mask)

    with jax.named_scope("gather_items"):
        for mask in (2, 6, 4):
            pieces[mask + 1] = swap(after(pieces[mask], named), "user", 1)
        own_items = [pieces[mask] for mask in range(n_user)]
        other_items = [swap(piece, "item", 1) for piece in own_items]

    with jax.named_scope("pack_tiles"):
        far_conf = pltpu.with_memory_space_constraint(conf, pltpu.HBM)
        given, packed = call(
            functools.partial(pack_kernel, slots),
            (
                pltpu.HBM((slot_total, half, block), jnp.int32),
                pltpu.HBM((near, 2 * slots * block + 8, block), jnp.int32),
            ),
            after(named, pieces[3]), far_conf, named, scalars=1, far=1, far_outs=2, limit=16,
            scratch=(
                pltpu.VMEM(conf.shape, jnp.int32),
                pltpu.SemaphoreType.DMA((slot_total,)),
                pltpu.SemaphoreType.DMA((slot_total + 1 + near,)),
            ),
        )
        other_named = swap(named, "item", 1)
        other_half = swap(given, "item", 1)

    with jax.named_scope("send_tiles"):
        halves = [list(range(start, start + near)) for start in (0, near)]
        tiles = lax.all_to_all(
            after(packed, *own_items), "user", 0, 0, tiled=True, axis_index_groups=halves
        )
        own_named = after(named, *own_items)

    with jax.named_scope("user_tiles"):
        columns = 2 * n_user * block
        dense = (shaped((rows, columns)), shaped((rows, columns), bf16))
        user_conf, user_weight = call(
            functools.partial(own_tiles_kernel, unobserved / (item_init.shape[0] * n_user * n_item)),
            dense, own_named, far_conf, scalars=1, far=1, flops=10 ** 9,
            scratch=(pltpu.VMEM((slot_total, half, block), jnp.int32), pltpu.SemaphoreType.DMA(())),
        )
        user_conf, user_weight = call(
            other_tiles_kernel, dense, other_named, other_half, user_conf, user_weight,
            scalars=1, flops=10 ** 9, aliases={2: 0, 3: 1},
        )

    def iterate(sides, confidence, pairs, both):
        work = 2 * sides[0].shape[0] * pairs.shape[0] * rank
        states = []
        for place, part in enumerate(sides):
            size = part.shape[0]
            state, begin = shaped(part.shape), place * size
            side, part = call(
                functools.partial(first_kernel, width, begin), (state, state),
                *both(part), confidence, pairs, flops=6 * work,
            )
            states.append((begin, state, (side,), part))
        for kernel in (second_kernel, third_kernel):
            for place, (begin, state, carried, part) in enumerate(states):
                last = shaped((8, state.shape[0])) if kernel is third_kernel else state
                *carried, part = call(
                    functools.partial(kernel, width, begin), (state, state, state, last),
                    *carried, *both(part), confidence, pairs, flops=6 * work,
                )
                states[place] = (begin, state, carried, part)
        return [value for _, _, carried, sums in states for value in (*carried, *both(sums))]

    state = shaped((rows, rank))
    with jax.named_scope("user_cg"):
        *sides, pairs = call(
            functools.partial(user_side_kernel, 2 * n_user),
            (shaped((rows // CHUNKS, rank)),) * CHUNKS + (shaped((columns, 2 * rank), bf16),),
            *own_items, *other_items, user_weight, flops=4 * rows * columns * rank,
        )
        shard = shaped((UB * half, rank))
        users, keep, give = call(
            user_last_kernel, (state, shard, shard),
            *iterate(sides, user_conf, pairs, others), flops=10 ** 6,
        )
        taken = swap(give, "item", 1)
        (user_factors,) = call(
            functools.partial(join_kernel, block), (shaped((UB * block, rank)),), keep, taken
        )

    with jax.named_scope("gather_users"):
        users, tiles = lax.optimization_barrier((users, tiles))
        found = [users, swap(users, "user", 1), swap(users, "user", 2)]

    with jax.named_scope("item_tiles"):
        lists = tiles[:, 2 * slots * block : 2 * slots * block + 2]
        columns = near * row_blocks * block
        item_conf, item_weight = call(
            functools.partial(
                item_tiles_kernel, unobserved / (user_factors.shape[0] * n_user * n_item), row_blocks, slots
            ),
            (shaped((2 * block, columns)), shaped((2 * block, columns), bf16)),
            lists, tiles, scalars=1, flops=10 ** 9,
        )

    with jax.named_scope("gather_users"):
        neighbour, item_conf = lax.optimization_barrier((found[2], item_conf))
        found.append(swap(neighbour, "user", 1))
        marks, ordered = [], []
        for mask, piece in enumerate(found):
            marks += [(mask, True), (mask, False)]
            ordered += [piece, swap(piece, "item", 1)]

    def both(value):
        return value, swap(value, "user", near)

    rows = 2 * block
    with jax.named_scope("item_cg"):
        *sides, pairs = call(
            functools.partial(item_side_kernel, row_blocks, block, marks),
            (shaped((rows // CHUNKS, rank)),) * CHUNKS + (shaped((columns, 2 * rank), bf16),),
            *ordered, item_weight, flops=4 * rows * columns * rank,
        )
        item_factors, unused = call(
            item_last_kernel, (shaped((block, rank)), shaped((rows, rank))),
            *iterate(sides, item_conf, pairs, both), flops=10 ** 6,
        )
    return (user_factors, item_factors)


def fits_dense(mesh):
    n_user, n_item = mesh.shape["user"], mesh.shape["item"]
    block = 128
    user_bytes = UB * n_item * block * n_user * block * 4
    return user_bytes <= DENSE_LIMIT and n_item % 2 == 0 and n_user == 8


def block_sum(slot_terms, block_ids, row_count, block_size):
    block_count = row_count // block_size
    targets = jnp.arange(block_count, dtype=jnp.int32)
    onehot = (block_ids[:, None] == targets[None, :]).astype(jnp.float32)
    summed = jnp.einsum("tr,tik->rik", onehot, slot_terms, precision=highest)
    return summed.reshape(row_count, slot_terms.shape[2])


def group_products(own_blocks, other_blocks, tile_values, own_ids, other_ids):
    own_rows = jnp.take(own_blocks, own_ids, axis=0)
    other_rows = jnp.take(other_blocks, other_ids, axis=0)
    scores = jnp.einsum("tik,tjk->tij", own_rows, other_rows, precision=highest)
    return jnp.einsum("tij,tjk->tik", scores * tile_values, other_rows, precision=highest)


def slot_products(own_blocks, other_blocks, tile_values, own_ids, other_ids):
    return group_products(own_blocks, other_blocks, tile_values, own_ids, other_ids)


def conjugate(right_side, apply_operator):
    solution = jnp.zeros_like(right_side)
    residual = right_side
    direction = right_side
    norm_now = jnp.sum(residual * residual, axis=-1, keepdims=True)
    for iteration in range(CG_ITERS):
        product_vec = apply_operator(direction)
        step_length = norm_now / jnp.sum(direction * product_vec, axis=-1, keepdims=True)
        solution = solution + step_length * direction
        residual = residual - step_length * product_vec
        norm_next = jnp.sum(residual * residual, axis=-1, keepdims=True)
        direction = residual + norm_next / norm_now * direction
        norm_now = norm_next
    return solution


def shards(item_init, tile_rows, tile_cols, tile_count, conf):
    slot_total = tile_rows.shape[-1]
    block_size = conf.shape[-1]
    factor_rank = item_init.shape[1]
    item_devices = lax.axis_size("item")
    user_devices = lax.axis_size("user")
    row_ids = tile_rows.reshape(slot_total)
    col_ids = tile_cols.reshape(slot_total)
    slot_count = tile_count.reshape(())
    counts = conf.reshape(slot_total, block_size, block_size).astype(jnp.float32)
    usable = (jnp.arange(slot_total, dtype=jnp.int32) < slot_count)[:, None, None]
    confidence = jnp.where(usable, counts, 0.0)
    weights = jnp.where(usable & (counts > 0.0), 1.0 + counts, 0.0)
    user_rows = UB * block_size
    item_rows = IB * block_size
    item_shard = lax.all_gather(item_init, "user", axis=0, tiled=True)
    item_blocks = item_shard.reshape(-1, block_size, factor_rank)
    item_gram = lax.psum(jnp.dot(item_init.T, item_init, precision=highest), ("user", "item"))
    user_weight = unobserved / (item_init.shape[0] * user_devices * item_devices)
    user_terms = jnp.einsum(
        "tij,tjk->tik", weights, jnp.take(item_blocks, col_ids, axis=0), precision=highest
    )
    user_side = lax.psum_scatter(
        block_sum(user_terms, row_ids, user_rows * lax.axis_size("item"), block_size),
        "item",
        scatter_dimension=0,
        tiled=True,
    )

    def user_operator(direction):
        shard_direction = lax.all_gather(direction, "item", axis=0, tiled=True)
        slot_terms = slot_products(
            shard_direction.reshape(-1, block_size, factor_rank),
            item_blocks,
            confidence,
            row_ids,
            col_ids,
        )
        summed = lax.psum_scatter(
            block_sum(slot_terms, row_ids, user_rows * lax.axis_size("item"), block_size),
            "item",
            scatter_dimension=0,
            tiled=True,
        )
        return (
            summed
            + user_weight * jnp.dot(direction, item_gram, precision=highest)
            + ridge * direction
        )

    user_factors = conjugate(user_side, user_operator)
    user_shard = lax.all_gather(user_factors, "item", axis=0, tiled=True)
    user_blocks = user_shard.reshape(-1, block_size, factor_rank)
    user_gram = lax.psum(jnp.dot(user_factors.T, user_factors, precision=highest), ("user", "item"))
    item_weight = unobserved / (user_factors.shape[0] * user_devices * item_devices)
    confidence_cols = jnp.swapaxes(confidence, 1, 2)
    slot_users = jnp.take(user_blocks, row_ids, axis=0)
    item_terms = jnp.einsum("tij,tik->tjk", weights, slot_users, precision=highest)
    item_side = lax.psum_scatter(
        block_sum(item_terms, col_ids, item_rows * lax.axis_size("user"), block_size),
        "user",
        scatter_dimension=0,
        tiled=True,
    )

    def item_operator(direction):
        shard_direction = lax.all_gather(direction, "user", axis=0, tiled=True)
        slot_terms = slot_products(
            shard_direction.reshape(-1, block_size, factor_rank),
            user_blocks,
            confidence_cols,
            col_ids,
            row_ids,
        )
        summed = lax.psum_scatter(
            block_sum(slot_terms, col_ids, item_rows * lax.axis_size("user"), block_size),
            "user",
            scatter_dimension=0,
            tiled=True,
        )
        return (
            summed
            + item_weight * jnp.dot(direction, user_gram, precision=highest)
            + ridge * direction
        )

    item_factors = conjugate(item_side, item_operator)
    return (user_factors, item_factors)


def solution(mesh):
    in_specs = (
        P(("item", "user"), None),
        P("user", "item", None),
        P("user", "item", None),
        P("user", "item"),
        P("user", "item", None, None, None),
    )
    out_specs = (P(("user", "item"), None), P(("item", "user"), None))
    program = dense_shards if fits_dense(mesh) else shards
    return jax.shard_map(program, mesh=mesh, in_specs=in_specs, out_specs=out_specs, check_vma=False)
```

```python
import functools
import math

import jax
import jax.numpy as jnp
from jax import lax
from jax.experimental import pallas as pl
from jax.experimental.pallas import tpu as pltpu
from jax.sharding import PartitionSpec as P

UB = 2
IB = 1
CG_ITERS = 3
CHUNKS = 2


highest = lax.Precision.HIGHEST
ridge = 5.0
unobserved = 256.0

f32 = jnp.float32
bf16 = jnp.bfloat16
MIB = 1 << 20
DENSE_LIMIT = 8 * MIB


def pair(value):
    high = value.astype(bf16)
    low = (value - high.astype(f32)).astype(bf16)
    return high, low


def row_sum(value):
    return jnp.sum(value, axis=-1, keepdims=True)


def split_rows(value):
    high, low = pair(value)
    return jnp.concatenate(
        [jnp.concatenate([high, low], axis=1), jnp.concatenate([low, high], axis=1)], axis=0
    )


def scores_of(lhs, factors):
    rows = lhs.shape[0] // 2
    both = lax.dot_general(lhs, factors, (((1,), (1,)), ((), ())), preferred_element_type=f32)
    return both[:rows] + both[rows:]


def tile_terms(direction, conf_ref, pairs_ref, width, begin):
    rows, rank = direction.shape
    lhs = split_rows(direction)
    total = jnp.zeros((rows, rank), f32)
    for start in range(0, conf_ref.shape[1], width):
        factors = pairs_ref[start : start + width, :]
        weighted = scores_of(lhs, factors) * conf_ref[begin : begin + rows, start : start + width]
        high, low = pair(weighted)
        out = jnp.dot(jnp.concatenate([high, low], axis=0), factors, preferred_element_type=f32)
        total = total + (
            (out[:rows, :rank] + out[:rows, rank:]) + (out[rows:, :rank] + out[rows:, rank:])
        )
    return total


def tile_squares(direction, conf_ref, pairs_ref, width, begin):
    rows, rank = direction.shape
    lhs = split_rows(direction)
    total = jnp.zeros((rows, rank), f32)
    for start in range(0, conf_ref.shape[1], width):
        scores = scores_of(lhs, pairs_ref[start : start + width, :])
        squares = scores * scores * conf_ref[begin : begin + rows, start : start + width]
        for part in range(0, width, rank):
            total = total + squares[:, part : part + rank]
    return total


def write_sides(weight_ref, pairs_ref, side_refs):
    rank = pairs_ref.shape[1] // 2
    both = jnp.dot(weight_ref[...], pairs_ref[...], preferred_element_type=f32)
    start = 0
    for side_ref in side_refs:
        rows = slice(start, start + side_ref.shape[0])
        side_ref[...] = both[rows, :rank] + both[rows, rank:]
        start += side_ref.shape[0]


def advance(solution, residual, direction, product):
    norm_now = row_sum(residual * residual)
    step_length = norm_now / row_sum(direction * product)
    solution = solution + step_length * direction
    residual = residual - step_length * product
    direction = residual + row_sum(residual * residual) / norm_now * direction
    return solution, residual, direction


def pack_kernel(slots, ids_ref, conf_ref, named_ref, given_ref, send_ref, held, in_sems, sems):
    slot_total, block, _ = conf_ref.shape
    half = block // 2
    owners = slot_total // slots
    near = owners // 2
    core = lax.rem(lax.axis_index("item"), 2)
    taken = [
        pltpu.make_async_copy(conf_ref.at[slot], held.at[slot], in_sems.at[slot]) for slot in range(slot_total)
    ]
    for copy in taken:
        copy.start()
    copies = []
    for owner in range(near):
        target = send_ref.at[owner, 2 * slots * block :, :]
        copies.append(pltpu.make_async_copy(named_ref, target, sems.at[len(copies)]))
        copies[-1].start()
    for slot in range(slot_total):
        owner = lax.rem(ids_ref[1, 0] + slot, owners)
        start = pl.multiple_of((owner // near * slots + slot // owners) * block, block)
        target = send_ref.at[lax.rem(owner, near), pl.ds(start, block), :]
        taken[slot].wait()
        copies.append(pltpu.make_async_copy(held.at[slot], target, sems.at[len(copies)]))
        copies[-1].start()
    rows = pl.ds(pl.multiple_of((1 - core) * half, half), half)
    copies.append(pltpu.make_async_copy(held.at[:, rows, :], given_ref, sems.at[len(copies)]))
    copies[-1].start()
    for copy in copies:
        copy.wait()


def user_tile(named_ref, slot, base, counts, dense_ref, weight_ref):
    half, block = counts.shape
    owners = dense_ref.shape[1] // block // 2
    owner = lax.rem(named_ref[1, 0] + slot, owners)
    row = pl.multiple_of(named_ref[0, slot] * half, half)
    col = pl.multiple_of((base + jnp.bitwise_xor(owner, lax.axis_index("user"))) * block, block)
    at = (pl.ds(row, half), pl.ds(col, block))
    value = counts.astype(f32)
    dense_ref[at] = dense_ref[at] + value
    weight_ref[at] = weight_ref[at] + jnp.where(value > 0.0, 1.0 + value, 0.0).astype(bf16)


def own_tiles_kernel(weight_zero, named_ref, conf_ref, dense_ref, weight_ref, held, sem):
    slot_total, block, _ = conf_ref.shape
    half = block // 2
    core = lax.rem(lax.axis_index("item"), 2)
    rows = pl.ds(pl.multiple_of(core * half, half), half)
    copy = pltpu.make_async_copy(conf_ref.at[:, rows, :], held, sem)
    copy.start()
    dense_ref[...] = jnp.full(dense_ref.shape, weight_zero, f32)
    weight_ref[...] = jnp.zeros(weight_ref.shape, bf16)
    copy.wait()

    def one(slot, carry):
        user_tile(named_ref, slot, 0, held[slot], dense_ref, weight_ref)
        return carry

    lax.fori_loop(0, jnp.minimum(named_ref[1, 1], slot_total), one, 0)


def other_tiles_kernel(named_ref, half_ref, dense_in, weight_in, dense_ref, weight_ref):
    slot_total, _, block = half_ref.shape
    owners = dense_ref.shape[1] // block // 2

    def one(slot, carry):
        user_tile(named_ref, slot, owners, half_ref[slot], dense_ref, weight_ref)
        return carry

    lax.fori_loop(0, jnp.minimum(named_ref[1, 1], slot_total), one, 0)


def user_side_kernel(count, *refs):
    pieces, (weight_ref, *side_refs, pairs_ref) = refs[:count], refs[count:]
    block = pairs_ref.shape[0] // count
    for place, piece in enumerate(pieces):
        high, low = pair(piece[:block, :])
        pairs_ref[place * block : (place + 1) * block, :] = jnp.concatenate([high, low], axis=1)
    write_sides(weight_ref, pairs_ref, side_refs)


def first_kernel(width, begin, own_ref, other_ref, conf_ref, pairs_ref, side_ref, out_ref):
    side = own_ref[...] + other_ref[...]
    side_ref[...] = side
    out_ref[...] = tile_terms(side, conf_ref, pairs_ref, width, begin)


def second_kernel(
    width, begin, side_ref, own_ref, other_ref, conf_ref, pairs_ref, x_ref, r_ref, d_ref, out_ref
):
    side = side_ref[...]
    product = own_ref[...] + other_ref[...] + ridge * side
    x, r, d = advance(jnp.zeros_like(side), side, side, product)
    x_ref[...] = x
    r_ref[...] = r
    d_ref[...] = d
    out_ref[...] = tile_terms(d, conf_ref, pairs_ref, width, begin)


def third_kernel(
    width, begin, x_in, r_in, d_in, own_ref, other_ref, conf_ref, pairs_ref, x_ref, r_ref, d_ref, sums_ref
):
    direction = d_in[...]
    product = own_ref[...] + other_ref[...] + ridge * direction
    x, r, d = advance(x_in[...], r_in[...], direction, product)
    x_ref[...] = x
    r_ref[...] = r
    d_ref[...] = d
    squares = tile_squares(d, conf_ref, pairs_ref, width, begin)
    ones = jnp.ones((8, squares.shape[1]), bf16)
    sums = jnp.zeros(sums_ref.shape, f32)
    for unused in range(3):
        part = squares.astype(bf16)
        squares = squares - part.astype(f32)
        sums = sums + lax.dot_general(ones, part, (((1,), (1,)), ((), ())), preferred_element_type=f32)
    sums_ref[...] = sums


def solve(refs, out_ref):
    start = 0
    for place in range(0, len(refs), 5):
        x_in, r_in, d_in, own_ref, other_ref = refs[place : place + 5]
        residual, direction = r_in[...], d_in[...]
        sums = jnp.transpose(own_ref[...] + other_ref[...])[:, :1]
        length = row_sum(residual * residual) / (sums + ridge * row_sum(direction * direction))
        out_ref[start : start + residual.shape[0], :] = x_in[...] + length * direction
        start += residual.shape[0]


def user_last_kernel(*refs):
    out_ref, keep_ref, give_ref = refs[-3:]
    solve(refs[:-3], out_ref)
    place = lax.axis_index("item")
    rows = keep_ref.shape[0]
    keep_ref[...] = out_ref[pl.ds(pl.multiple_of(place * rows, rows), rows), :]
    other = jnp.bitwise_xor(place, 1)
    give_ref[...] = out_ref[pl.ds(pl.multiple_of(other * rows, rows), rows), :]


def item_tiles_kernel(weight_zero, row_blocks, slots, lists_ref, tiles_ref, dense_ref, weight_ref):
    near = tiles_ref.shape[0]
    block = tiles_ref.shape[2]
    me = lax.rem(lax.axis_index("user"), near)
    dense_ref[...] = jnp.full(dense_ref.shape, weight_zero, f32)
    weight_ref[...] = jnp.zeros(weight_ref.shape, bf16)
    for source in range(near):
        mask = jnp.bitwise_xor(source, me)
        for upper in range(2):
            first = lax.rem(me + upper * near - lists_ref[source, 1, 0] + 2 * near, 2 * near)
            for slot in range(slots):
                start = (upper * slots + slot) * block
                place = first + 2 * near * slot
                used = place < lists_ref[source, 1, 1]
                tile = jnp.where(used, tiles_ref[source, start : start + block, :], 0)
                value = jnp.transpose(tile.astype(f32))
                row = lists_ref[source, 0, place]
                col = pl.multiple_of((mask * row_blocks + row) * block, block)
                at = (slice(upper * block, (upper + 1) * block), pl.ds(col, block))
                dense_ref[at] = dense_ref[at] + value
                weight_ref[at] = weight_ref[at] + jnp.where(value > 0.0, 1.0 + value, 0.0).astype(bf16)


def join_kernel(block, own_ref, other_ref, out_ref):
    half = block // 2
    core = lax.rem(lax.axis_index("item"), 2)
    for start in range(0, out_ref.shape[0], block):
        for offset, part_ref in ((core, own_ref), (1 - core, other_ref)):
            rows = pl.ds(pl.multiple_of(start + offset * half, half), half)
            out_ref[rows, :] = part_ref[start // 2 : start // 2 + half, :]


def item_side_kernel(row_blocks, block, marks, *refs):
    pieces, (weight_ref, *side_refs, pairs_ref) = refs[: len(marks)], refs[len(marks) :]
    half = block // 2
    core = lax.rem(lax.axis_index("item"), 2)
    for (mask, own_half), piece in zip(marks, pieces):
        offset = pl.multiple_of((core if own_half else 1 - core) * half, half)
        for row in range(row_blocks):
            high, low = pair(piece[row * half : (row + 1) * half, :])
            start = (mask * row_blocks + row) * block
            pairs_ref[pl.ds(start + offset, half), :] = jnp.concatenate([high, low], axis=1)
    write_sides(weight_ref, pairs_ref, side_refs)


def item_last_kernel(*refs):
    out_ref, all_ref = refs[-2:]
    solve(refs[:-2], all_ref)
    rows = out_ref.shape[0]
    upper = lax.axis_index("user") // (lax.axis_size("user") // 2)
    out_ref[...] = all_ref[pl.ds(pl.multiple_of(upper * rows, rows), rows), :]


VMEM = pltpu.VMEM
SMEM = pltpu.SMEM


def call(kernel, outs, *operands, scalars=0, far=0, far_outs=0, flops=0, scratch=(), limit=16, aliases=None):
    size = sum(op.size * op.dtype.itemsize for op in operands)
    size += sum(4 * math.prod(out.shape) for out in outs)
    spaces = [SMEM] * scalars + [pl.ANY] * far + [VMEM] * (len(operands) - scalars - far)
    return pl.pallas_call(
        kernel,
        out_shape=tuple(outs),
        in_specs=[pl.BlockSpec(memory_space=space) for space in spaces],
        out_specs=tuple(pl.BlockSpec(memory_space=pl.ANY if place < far_outs else VMEM) for place in range(len(outs))),
        scratch_shapes=scratch,
        input_output_aliases=aliases or {},
        compiler_params=pltpu.CompilerParams(vmem_limit_bytes=limit * MIB),
        cost_estimate=pl.CostEstimate(flops=flops, bytes_accessed=size, transcendentals=0),
    )(*operands)


def shaped(shape, dtype=f32):
    return jax.ShapeDtypeStruct(shape, dtype)


def dense_shards(item_init, tile_rows, tile_cols, tile_count, conf):
    slot_total = tile_rows.shape[-1]
    block, rank = conf.shape[-1], item_init.shape[1]
    half = block // 2
    n_item, n_user = lax.axis_size("item"), lax.axis_size("user")
    row_blocks = UB * n_item
    rows = row_blocks * half
    slots = -(-slot_total // n_user)
    width = 4 * rank
    def swap(value, axis, mask):
        size = n_item if axis == "item" else n_user
        return lax.ppermute(value, axis, [(place, place ^ mask) for place in range(size)])

    def others(value):
        total = value
        mask = 2
        while mask < n_item:
            moved = swap(total, "item", mask)
            if mask * 2 >= n_item:
                return total, moved
            total = total + moved
            mask *= 2

    conf = conf.reshape(slot_total, block, block)
    def after(value, *tokens):
        return lax.optimization_barrier((value, *tokens))[0]

    named = sum(
        jnp.pad(value.reshape(1, -1), ((row, 7 - row), (lane, rank - lane - size)))
        for value, row, lane, size in (
            (tile_rows, 0, 0, slot_total), (tile_cols[..., :1], 1, 0, 1), (tile_count, 1, 1, 1)
        )
    )
    near = n_user // 2
    with jax.named_scope("gather_items"):
        pieces = {0: item_init}
        for mask in (6, 4, 2, 1):
            pieces[mask] = swap(item_init, "user", mask)

    with jax.named_scope("gather_items"):
        for mask in (2, 6, 4):
            pieces[mask + 1] = swap(after(pieces[mask], named), "user", 1)
        own_items = [pieces[mask] for mask in range(n_user)]
        other_items = [swap(piece, "item", 1) for piece in own_items]

    with jax.named_scope("pack_tiles"):
        far_conf = pltpu.with_memory_space_constraint(conf, pltpu.HBM)
        given, packed = call(
            functools.partial(pack_kernel, slots),
            (
                pltpu.HBM((slot_total, half, block), jnp.int32),
                pltpu.HBM((near, 2 * slots * block + 8, block), jnp.int32),
            ),
            after(named, pieces[3]), far_conf, named, scalars=1, far=1, far_outs=2, limit=16,
            scratch=(
                pltpu.VMEM(conf.shape, jnp.int32),
                pltpu.SemaphoreType.DMA((slot_total,)),
                pltpu.SemaphoreType.DMA((slot_total + 1 + near,)),
            ),
        )
        other_named = swap(named, "item", 1)
        other_half = swap(given, "item", 1)

    with jax.named_scope("send_tiles"):
        halves = [list(range(start, start + near)) for start in (0, near)]
        tiles = lax.all_to_all(
            after(packed, *own_items), "user", 0, 0, tiled=True, axis_index_groups=halves
        )
        own_named = after(named, *own_items)

    with jax.named_scope("user_tiles"):
        columns = 2 * n_user * block
        dense = (shaped((rows, columns)), shaped((rows, columns), bf16))
        user_conf, user_weight = call(
            functools.partial(own_tiles_kernel, unobserved / (item_init.shape[0] * n_user * n_item)),
            dense, own_named, far_conf, scalars=1, far=1, flops=10 ** 9,
            scratch=(pltpu.VMEM((slot_total, half, block), jnp.int32), pltpu.SemaphoreType.DMA(())),
        )
        user_conf, user_weight = call(
            other_tiles_kernel, dense, other_named, other_half, user_conf, user_weight,
            scalars=1, flops=10 ** 9, aliases={2: 0, 3: 1},
        )

    def iterate(sides, confidence, pairs, both):
        work = 2 * sides[0].shape[0] * pairs.shape[0] * rank
        states = []
        for place, part in enumerate(sides):
            size = part.shape[0]
            state, begin = shaped(part.shape), place * size
            side, part = call(
                functools.partial(first_kernel, width, begin), (state, state),
                *both(part), confidence, pairs, flops=6 * work,
            )
            states.append((begin, state, (side,), part))
        for kernel in (second_kernel, third_kernel):
            for place, (begin, state, carried, part) in enumerate(states):
                last = shaped((8, state.shape[0])) if kernel is third_kernel else state
                *carried, part = call(
                    functools.partial(kernel, width, begin), (state, state, state, last),
                    *carried, *both(part), confidence, pairs, flops=6 * work,
                )
                states[place] = (begin, state, carried, part)
        return [value for _, _, carried, sums in states for value in (*carried, *both(sums))]

    state = shaped((rows, rank))
    with jax.named_scope("user_cg"):
        *sides, pairs = call(
            functools.partial(user_side_kernel, 2 * n_user),
            (shaped((rows // CHUNKS, rank)),) * CHUNKS + (shaped((columns, 2 * rank), bf16),),
            *own_items, *other_items, user_weight, flops=4 * rows * columns * rank,
        )
        shard = shaped((UB * half, rank))
        users, keep, give = call(
            user_last_kernel, (state, shard, shard),
            *iterate(sides, user_conf, pairs, others), flops=10 ** 6,
        )
        taken = swap(give, "item", 1)
        (user_factors,) = call(
            functools.partial(join_kernel, block), (shaped((UB * block, rank)),), keep, taken
        )

    with jax.named_scope("gather_users"):
        users, tiles = lax.optimization_barrier((users, tiles))
        found = [users, swap(users, "user", 1), swap(users, "user", 2)]

    with jax.named_scope("item_tiles"):
        lists = tiles[:, 2 * slots * block : 2 * slots * block + 2]
        columns = near * row_blocks * block
        item_conf, item_weight = call(
            functools.partial(
                item_tiles_kernel, unobserved / (user_factors.shape[0] * n_user * n_item), row_blocks, slots
            ),
            (shaped((2 * block, columns)), shaped((2 * block, columns), bf16)),
            lists, tiles, scalars=1, flops=10 ** 9,
        )

    with jax.named_scope("gather_users"):
        neighbour, item_conf = lax.optimization_barrier((found[2], item_conf))
        found.append(swap(neighbour, "user", 1))
        marks, ordered = [], []
        for mask, piece in enumerate(found):
            marks += [(mask, True), (mask, False)]
            ordered += [piece, swap(piece, "item", 1)]

    def both(value):
        return value, swap(value, "user", near)

    rows = 2 * block
    with jax.named_scope("item_cg"):
        *sides, pairs = call(
            functools.partial(item_side_kernel, row_blocks, block, marks),
            (shaped((rows // CHUNKS, rank)),) * CHUNKS + (shaped((columns, 2 * rank), bf16),),
            *ordered, item_weight, flops=4 * rows * columns * rank,
        )
        item_factors, unused = call(
            item_last_kernel, (shaped((block, rank)), shaped((rows, rank))),
            *iterate(sides, item_conf, pairs, both), flops=10 ** 6,
        )
    return (user_factors, item_factors)


def fits_dense(mesh):
    n_user, n_item = mesh.shape["user"], mesh.shape["item"]
    block = 128
    user_bytes = UB * n_item * block * n_user * block * 4
    return user_bytes <= DENSE_LIMIT and n_item % 2 == 0 and n_user == 8


def block_sum(slot_terms, block_ids, row_count, block_size):
    block_count = row_count // block_size
    targets = jnp.arange(block_count, dtype=jnp.int32)
    onehot = (block_ids[:, None] == targets[None, :]).astype(jnp.float32)
    summed = jnp.einsum("tr,tik->rik", onehot, slot_terms, precision=highest)
    return summed.reshape(row_count, slot_terms.shape[2])


def group_products(own_blocks, other_blocks, tile_values, own_ids, other_ids):
    own_rows = jnp.take(own_blocks, own_ids, axis=0)
    other_rows = jnp.take(other_blocks, other_ids, axis=0)
    scores = jnp.einsum("tik,tjk->tij", own_rows, other_rows, precision=highest)
    return jnp.einsum("tij,tjk->tik", scores * tile_values, other_rows, precision=highest)


def slot_products(own_blocks, other_blocks, tile_values, own_ids, other_ids):
    return group_products(own_blocks, other_blocks, tile_values, own_ids, other_ids)


def conjugate(right_side, apply_operator):
    solution = jnp.zeros_like(right_side)
    residual = right_side
    direction = right_side
    norm_now = jnp.sum(residual * residual, axis=-1, keepdims=True)
    for iteration in range(CG_ITERS):
        product_vec = apply_operator(direction)
        step_length = norm_now / jnp.sum(direction * product_vec, axis=-1, keepdims=True)
        solution = solution + step_length * direction
        residual = residual - step_length * product_vec
        norm_next = jnp.sum(residual * residual, axis=-1, keepdims=True)
        direction = residual + norm_next / norm_now * direction
        norm_now = norm_next
    return solution


def shards(item_init, tile_rows, tile_cols, tile_count, conf):
    slot_total = tile_rows.shape[-1]
    block_size = conf.shape[-1]
    factor_rank = item_init.shape[1]
    item_devices = lax.axis_size("item")
    user_devices = lax.axis_size("user")
    row_ids = tile_rows.reshape(slot_total)
    col_ids = tile_cols.reshape(slot_total)
    slot_count = tile_count.reshape(())
    counts = conf.reshape(slot_total, block_size, block_size).astype(jnp.float32)
    usable = (jnp.arange(slot_total, dtype=jnp.int32) < slot_count)[:, None, None]
    confidence = jnp.where(usable, counts, 0.0)
    weights = jnp.where(usable & (counts > 0.0), 1.0 + counts, 0.0)
    user_rows = UB * block_size
    item_rows = IB * block_size
    item_shard = lax.all_gather(item_init, "user", axis=0, tiled=True)
    item_blocks = item_shard.reshape(-1, block_size, factor_rank)
    item_gram = lax.psum(jnp.dot(item_init.T, item_init, precision=highest), ("user", "item"))
    user_weight = unobserved / (item_init.shape[0] * user_devices * item_devices)
    user_terms = jnp.einsum(
        "tij,tjk->tik", weights, jnp.take(item_blocks, col_ids, axis=0), precision=highest
    )
    user_side = lax.psum_scatter(
        block_sum(user_terms, row_ids, user_rows * lax.axis_size("item"), block_size),
        "item",
        scatter_dimension=0,
        tiled=True,
    )

    def user_operator(direction):
        shard_direction = lax.all_gather(direction, "item", axis=0, tiled=True)
        slot_terms = slot_products(
            shard_direction.reshape(-1, block_size, factor_rank),
            item_blocks,
            confidence,
            row_ids,
            col_ids,
        )
        summed = lax.psum_scatter(
            block_sum(slot_terms, row_ids, user_rows * lax.axis_size("item"), block_size),
            "item",
            scatter_dimension=0,
            tiled=True,
        )
        return (
            summed
            + user_weight * jnp.dot(direction, item_gram, precision=highest)
            + ridge * direction
        )

    user_factors = conjugate(user_side, user_operator)
    user_shard = lax.all_gather(user_factors, "item", axis=0, tiled=True)
    user_blocks = user_shard.reshape(-1, block_size, factor_rank)
    user_gram = lax.psum(jnp.dot(user_factors.T, user_factors, precision=highest), ("user", "item"))
    item_weight = unobserved / (user_factors.shape[0] * user_devices * item_devices)
    confidence_cols = jnp.swapaxes(confidence, 1, 2)
    slot_users = jnp.take(user_blocks, row_ids, axis=0)
    item_terms = jnp.einsum("tij,tik->tjk", weights, slot_users, precision=highest)
    item_side = lax.psum_scatter(
        block_sum(item_terms, col_ids, item_rows * lax.axis_size("user"), block_size),
        "user",
        scatter_dimension=0,
        tiled=True,
    )

    def item_operator(direction):
        shard_direction = lax.all_gather(direction, "user", axis=0, tiled=True)
        slot_terms = slot_products(
            shard_direction.reshape(-1, block_size, factor_rank),
            user_blocks,
            confidence_cols,
            col_ids,
            row_ids,
        )
        summed = lax.psum_scatter(
            block_sum(slot_terms, col_ids, item_rows * lax.axis_size("user"), block_size),
            "user",
            scatter_dimension=0,
            tiled=True,
        )
        return (
            summed
            + item_weight * jnp.dot(direction, user_gram, precision=highest)
            + ridge * direction
        )

    item_factors = conjugate(item_side, item_operator)
    return (user_factors, item_factors)


def solution(mesh):
    in_specs = (
        P(("item", "user"), None),
        P("user", "item", None),
        P("user", "item", None),
        P("user", "item"),
        P("user", "item", None, None, None),
    )
    out_specs = (P(("user", "item"), None), P(("item", "user"), None))
    program = dense_shards if fits_dense(mesh) else shards
    return jax.shard_map(program, mesh=mesh, in_specs=in_specs, out_specs=out_specs, check_vma=False)
```

```python
import functools
import math

import jax
import jax.numpy as jnp
from jax import lax
from jax.experimental import pallas as pl
from jax.experimental.pallas import tpu as pltpu
from jax.sharding import PartitionSpec as P

UB = 2
IB = 1
CG_ITERS = 3
CHUNKS = 2


highest = lax.Precision.HIGHEST
ridge = 5.0
unobserved = 256.0

f32 = jnp.float32
bf16 = jnp.bfloat16
MIB = 1 << 20
DENSE_LIMIT = 8 * MIB


def pair(value):
    high = value.astype(bf16)
    low = (value - high.astype(f32)).astype(bf16)
    return high, low


def row_sum(value):
    return jnp.sum(value, axis=-1, keepdims=True)


def split_rows(value):
    high, low = pair(value)
    return jnp.concatenate(
        [jnp.concatenate([high, low], axis=1), jnp.concatenate([low, high], axis=1)], axis=0
    )


def scores_of(lhs, factors):
    rows = lhs.shape[0] // 2
    both = lax.dot_general(lhs, factors, (((1,), (1,)), ((), ())), preferred_element_type=f32)
    return both[:rows] + both[rows:]


def tile_terms(direction, conf_ref, pairs_ref, width, begin):
    rows, rank = direction.shape
    lhs = split_rows(direction)
    total = jnp.zeros((rows, rank), f32)
    for start in range(0, conf_ref.shape[1], width):
        factors = pairs_ref[start : start + width, :]
        weighted = scores_of(lhs, factors) * conf_ref[begin : begin + rows, start : start + width]
        high, low = pair(weighted)
        out = jnp.dot(jnp.concatenate([high, low], axis=0), factors, preferred_element_type=f32)
        total = total + (
            (out[:rows, :rank] + out[:rows, rank:]) + (out[rows:, :rank] + out[rows:, rank:])
        )
    return total


def tile_squares(direction, conf_ref, pairs_ref, width, begin):
    rows, rank = direction.shape
    lhs = split_rows(direction)
    total = jnp.zeros((rows, rank), f32)
    for start in range(0, conf_ref.shape[1], width):
        scores = scores_of(lhs, pairs_ref[start : start + width, :])
        squares = scores * scores * conf_ref[begin : begin + rows, start : start + width]
        for part in range(0, width, rank):
            total = total + squares[:, part : part + rank]
    return total


def write_sides(weight_ref, pairs_ref, side_refs):
    rank = pairs_ref.shape[1] // 2
    both = jnp.dot(weight_ref[...], pairs_ref[...], preferred_element_type=f32)
    start = 0
    for side_ref in side_refs:
        rows = slice(start, start + side_ref.shape[0])
        side_ref[...] = both[rows, :rank] + both[rows, rank:]
        start += side_ref.shape[0]


def advance(solution, residual, direction, product):
    norm_now = row_sum(residual * residual)
    step_length = norm_now / row_sum(direction * product)
    solution = solution + step_length * direction
    residual = residual - step_length * product
    direction = residual + row_sum(residual * residual) / norm_now * direction
    return solution, residual, direction


def pack_kernel(slots, ids_ref, conf_ref, named_ref, given_ref, send_ref, held, in_sems, sems):
    slot_total, block, _ = conf_ref.shape
    half = block // 2
    owners = slot_total // slots
    near = owners // 2
    core = lax.rem(lax.axis_index("item"), 2)
    taken = [
        pltpu.make_async_copy(conf_ref.at[slot], held.at[slot], in_sems.at[slot]) for slot in range(slot_total)
    ]
    for copy in taken:
        copy.start()
    copies = []
    for owner in range(near):
        target = send_ref.at[owner, 2 * slots * block :, :]
        copies.append(pltpu.make_async_copy(named_ref, target, sems.at[len(copies)]))
        copies[-1].start()
    for slot in range(slot_total):
        owner = lax.rem(ids_ref[1, 0] + slot, owners)
        start = pl.multiple_of((owner // near * slots + slot // owners) * block, block)
        target = send_ref.at[lax.rem(owner, near), pl.ds(start, block), :]
        taken[slot].wait()
        copies.append(pltpu.make_async_copy(held.at[slot], target, sems.at[len(copies)]))
        copies[-1].start()
    rows = pl.ds(pl.multiple_of((1 - core) * half, half), half)
    copies.append(pltpu.make_async_copy(held.at[:, rows, :], given_ref, sems.at[len(copies)]))
    copies[-1].start()
    for copy in copies:
        copy.wait()


def user_tile(named_ref, slot, base, counts, dense_ref, weight_ref):
    half, block = counts.shape
    owners = dense_ref.shape[1] // block // 2
    owner = lax.rem(named_ref[1, 0] + slot, owners)
    row = pl.multiple_of(named_ref[0, slot] * half, half)
    col = pl.multiple_of((base + jnp.bitwise_xor(owner, lax.axis_index("user"))) * block, block)
    at = (pl.ds(row, half), pl.ds(col, block))
    value = counts.astype(f32)
    dense_ref[at] = dense_ref[at] + value
    weight_ref[at] = weight_ref[at] + jnp.where(value > 0.0, 1.0 + value, 0.0).astype(bf16)


def own_tiles_kernel(weight_zero, named_ref, conf_ref, dense_ref, weight_ref, held, sem):
    slot_total, block, _ = conf_ref.shape
    half = block // 2
    core = lax.rem(lax.axis_index("item"), 2)
    rows = pl.ds(pl.multiple_of(core * half, half), half)
    step = slot_total // sem.shape[0]
    copies = []
    for place in range(sem.shape[0]):
        slots = pl.ds(place * step, step)
        copies.append(pltpu.make_async_copy(conf_ref.at[slots, rows, :], held.at[slots], sem.at[place]))
        copies[-1].start()
    dense_ref[...] = jnp.full(dense_ref.shape, weight_zero, f32)
    weight_ref[...] = jnp.zeros(weight_ref.shape, bf16)
    for slot in range(slot_total):
        if slot % step == 0:
            copies[slot // step].wait()
        counts = jnp.where(slot < named_ref[1, 1], held[slot], 0)
        user_tile(named_ref, slot, 0, counts, dense_ref, weight_ref)


def other_tiles_kernel(named_ref, half_ref, dense_in, weight_in, dense_ref, weight_ref):
    slot_total, _, block = half_ref.shape
    owners = dense_ref.shape[1] // block // 2

    for slot in range(slot_total):
        counts = jnp.where(slot < named_ref[1, 1], half_ref[slot], 0)
        user_tile(named_ref, slot, owners, counts, dense_ref, weight_ref)


def user_side_kernel(count, *refs):
    pieces, (weight_ref, *side_refs, pairs_ref) = refs[:count], refs[count:]
    block = pairs_ref.shape[0] // count
    for place, piece in enumerate(pieces):
        high, low = pair(piece[:block, :])
        pairs_ref[place * block : (place + 1) * block, :] = jnp.concatenate([high, low], axis=1)
    write_sides(weight_ref, pairs_ref, side_refs)


def first_kernel(width, begin, own_ref, other_ref, conf_ref, pairs_ref, side_ref, out_ref):
    side = own_ref[...] + other_ref[...]
    side_ref[...] = side
    out_ref[...] = tile_terms(side, conf_ref, pairs_ref, width, begin)


def second_kernel(
    width, begin, side_ref, own_ref, other_ref, conf_ref, pairs_ref, x_ref, r_ref, d_ref, out_ref
):
    side = side_ref[...]
    product = own_ref[...] + other_ref[...] + ridge * side
    x, r, d = advance(jnp.zeros_like(side), side, side, product)
    x_ref[...] = x
    r_ref[...] = r
    d_ref[...] = d
    out_ref[...] = tile_terms(d, conf_ref, pairs_ref, width, begin)


def third_kernel(
    width, begin, x_in, r_in, d_in, own_ref, other_ref, conf_ref, pairs_ref, x_ref, r_ref, d_ref, sums_ref
):
    direction = d_in[...]
    product = own_ref[...] + other_ref[...] + ridge * direction
    x, r, d = advance(x_in[...], r_in[...], direction, product)
    x_ref[...] = x
    r_ref[...] = r
    d_ref[...] = d
    squares = tile_squares(d, conf_ref, pairs_ref, width, begin)
    ones = jnp.ones((8, squares.shape[1]), bf16)
    sums = jnp.zeros(sums_ref.shape, f32)
    for unused in range(3):
        part = squares.astype(bf16)
        squares = squares - part.astype(f32)
        sums = sums + lax.dot_general(ones, part, (((1,), (1,)), ((), ())), preferred_element_type=f32)
    sums_ref[...] = sums


def solve(refs, out_ref):
    start = 0
    for place in range(0, len(refs), 5):
        x_in, r_in, d_in, own_ref, other_ref = refs[place : place + 5]
        residual, direction = r_in[...], d_in[...]
        sums = jnp.transpose(own_ref[...] + other_ref[...])[:, :1]
        length = row_sum(residual * residual) / (sums + ridge * row_sum(direction * direction))
        out_ref[start : start + residual.shape[0], :] = x_in[...] + length * direction
        start += residual.shape[0]


def user_last_kernel(*refs):
    out_ref, keep_ref, give_ref = refs[-3:]
    solve(refs[:-3], out_ref)
    place = lax.axis_index("item")
    rows = keep_ref.shape[0]
    keep_ref[...] = out_ref[pl.ds(pl.multiple_of(place * rows, rows), rows), :]
    other = jnp.bitwise_xor(place, 1)
    give_ref[...] = out_ref[pl.ds(pl.multiple_of(other * rows, rows), rows), :]


def item_tiles_kernel(weight_zero, row_blocks, slots, lists_ref, tiles_ref, dense_ref, weight_ref):
    near = tiles_ref.shape[0]
    block = tiles_ref.shape[2]
    me = lax.rem(lax.axis_index("user"), near)
    dense_ref[...] = jnp.full(dense_ref.shape, weight_zero, f32)
    weight_ref[...] = jnp.zeros(weight_ref.shape, bf16)
    for source in range(near):
        mask = jnp.bitwise_xor(source, me)
        for upper in range(2):
            first = lax.rem(me + upper * near - lists_ref[source, 1, 0] + 2 * near, 2 * near)
            for slot in range(slots):
                start = (upper * slots + slot) * block
                place = first + 2 * near * slot
                used = place < lists_ref[source, 1, 1]
                tile = jnp.where(used, tiles_ref[source, start : start + block, :], 0)
                value = jnp.transpose(tile.astype(f32))
                row = lists_ref[source, 0, place]
                col = pl.multiple_of((mask * row_blocks + row) * block, block)
                at = (slice(upper * block, (upper + 1) * block), pl.ds(col, block))
                dense_ref[at] = dense_ref[at] + value
                weight_ref[at] = weight_ref[at] + jnp.where(value > 0.0, 1.0 + value, 0.0).astype(bf16)


def join_kernel(block, own_ref, other_ref, out_ref):
    half = block // 2
    core = lax.rem(lax.axis_index("item"), 2)
    for start in range(0, out_ref.shape[0], block):
        for offset, part_ref in ((core, own_ref), (1 - core, other_ref)):
            rows = pl.ds(pl.multiple_of(start + offset * half, half), half)
            out_ref[rows, :] = part_ref[start // 2 : start // 2 + half, :]


def item_side_kernel(row_blocks, block, marks, *refs):
    pieces, (weight_ref, *side_refs, pairs_ref) = refs[: len(marks)], refs[len(marks) :]
    half = block // 2
    core = lax.rem(lax.axis_index("item"), 2)
    for (mask, own_half), piece in zip(marks, pieces):
        offset = pl.multiple_of((core if own_half else 1 - core) * half, half)
        for row in range(row_blocks):
            high, low = pair(piece[row * half : (row + 1) * half, :])
            start = (mask * row_blocks + row) * block
            pairs_ref[pl.ds(start + offset, half), :] = jnp.concatenate([high, low], axis=1)
    write_sides(weight_ref, pairs_ref, side_refs)


def item_last_kernel(*refs):
    out_ref, all_ref = refs[-2:]
    solve(refs[:-2], all_ref)
    rows = out_ref.shape[0]
    upper = lax.axis_index("user") // (lax.axis_size("user") // 2)
    out_ref[...] = all_ref[pl.ds(pl.multiple_of(upper * rows, rows), rows), :]


VMEM = pltpu.VMEM
SMEM = pltpu.SMEM


def call(kernel, outs, *operands, scalars=0, far=0, far_outs=0, flops=0, scratch=(), limit=16, aliases=None):
    size = sum(op.size * op.dtype.itemsize for op in operands)
    size += sum(4 * math.prod(out.shape) for out in outs)
    spaces = [SMEM] * scalars + [pl.ANY] * far + [VMEM] * (len(operands) - scalars - far)
    return pl.pallas_call(
        kernel,
        out_shape=tuple(outs),
        in_specs=[pl.BlockSpec(memory_space=space) for space in spaces],
        out_specs=tuple(pl.BlockSpec(memory_space=pl.ANY if place < far_outs else VMEM) for place in range(len(outs))),
        scratch_shapes=scratch,
        input_output_aliases=aliases or {},
        compiler_params=pltpu.CompilerParams(vmem_limit_bytes=limit * MIB),
        cost_estimate=pl.CostEstimate(flops=flops, bytes_accessed=size, transcendentals=0),
    )(*operands)


def shaped(shape, dtype=f32):
    return jax.ShapeDtypeStruct(shape, dtype)


def dense_shards(item_init, tile_rows, tile_cols, tile_count, conf):
    slot_total = tile_rows.shape[-1]
    block, rank = conf.shape[-1], item_init.shape[1]
    half = block // 2
    n_item, n_user = lax.axis_size("item"), lax.axis_size("user")
    row_blocks = UB * n_item
    rows = row_blocks * half
    slots = -(-slot_total // n_user)
    width = 4 * rank
    def swap(value, axis, mask):
        size = n_item if axis == "item" else n_user
        return lax.ppermute(value, axis, [(place, place ^ mask) for place in range(size)])

    def others(value):
        total = value
        mask = 2
        while mask < n_item:
            moved = swap(total, "item", mask)
            if mask * 2 >= n_item:
                return total, moved
            total = total + moved
            mask *= 2

    conf = conf.reshape(slot_total, block, block)
    def after(value, *tokens):
        return lax.optimization_barrier((value, *tokens))[0]

    named = sum(
        jnp.pad(value.reshape(1, -1), ((row, 7 - row), (lane, rank - lane - size)))
        for value, row, lane, size in (
            (tile_rows, 0, 0, slot_total), (tile_cols[..., :1], 1, 0, 1), (tile_count, 1, 1, 1)
        )
    )
    near = n_user // 2
    with jax.named_scope("gather_items"):
        pieces = {0: item_init}
        for mask in (6, 4, 2, 1):
            pieces[mask] = swap(item_init, "user", mask)

    with jax.named_scope("gather_items"):
        for mask in (2, 6, 4):
            pieces[mask + 1] = swap(after(pieces[mask], named), "user", 1)
        own_items = [pieces[mask] for mask in range(n_user)]
        other_items = [swap(piece, "item", 1) for piece in own_items]

    with jax.named_scope("pack_tiles"):
        far_conf = pltpu.with_memory_space_constraint(conf, pltpu.HBM)
        given, packed = call(
            functools.partial(pack_kernel, slots),
            (
                pltpu.HBM((slot_total, half, block), jnp.int32),
                pltpu.HBM((near, 2 * slots * block + 8, block), jnp.int32),
            ),
            after(named, pieces[3]), far_conf, named, scalars=1, far=1, far_outs=2, limit=16,
            scratch=(
                pltpu.VMEM(conf.shape, jnp.int32),
                pltpu.SemaphoreType.DMA((slot_total,)),
                pltpu.SemaphoreType.DMA((slot_total + 1 + near,)),
            ),
        )
        other_named = swap(named, "item", 1)
        other_half = swap(given, "item", 1)

    with jax.named_scope("send_tiles"):
        halves = [list(range(start, start + near)) for start in (0, near)]
        tiles = lax.all_to_all(
            after(packed, *own_items), "user", 0, 0, tiled=True, axis_index_groups=halves
        )
        own_named = after(named, *own_items)

    with jax.named_scope("user_tiles"):
        columns = 2 * n_user * block
        dense = (shaped((rows, columns)), shaped((rows, columns), bf16))
        user_conf, user_weight = call(
            functools.partial(own_tiles_kernel, unobserved / (item_init.shape[0] * n_user * n_item)),
            dense, own_named, far_conf, scalars=1, far=1, flops=10 ** 9,
            scratch=(pltpu.VMEM((slot_total, half, block), jnp.int32), pltpu.SemaphoreType.DMA((8,))),
        )
        user_conf, user_weight = call(
            other_tiles_kernel, dense, other_named, other_half, user_conf, user_weight,
            scalars=1, flops=10 ** 9, aliases={2: 0, 3: 1},
        )

    def iterate(sides, confidence, pairs, both):
        work = 2 * sides[0].shape[0] * pairs.shape[0] * rank
        states = []
        for place, part in enumerate(sides):
            size = part.shape[0]
            state, begin = shaped(part.shape), place * size
            side, part = call(
                functools.partial(first_kernel, width, begin), (state, state),
                *both(part), confidence, pairs, flops=6 * work,
            )
            states.append((begin, state, (side,), part))
        for kernel in (second_kernel, third_kernel):
            for place, (begin, state, carried, part) in enumerate(states):
                last = shaped((8, state.shape[0])) if kernel is third_kernel else state
                *carried, part = call(
                    functools.partial(kernel, width, begin), (state, state, state, last),
                    *carried, *both(part), confidence, pairs, flops=6 * work,
                )
                states[place] = (begin, state, carried, part)
        return [value for _, _, carried, sums in states for value in (*carried, *both(sums))]

    state = shaped((rows, rank))
    with jax.named_scope("user_cg"):
        *sides, pairs = call(
            functools.partial(user_side_kernel, 2 * n_user),
            (shaped((rows // CHUNKS, rank)),) * CHUNKS + (shaped((columns, 2 * rank), bf16),),
            *own_items, *other_items, user_weight, flops=4 * rows * columns * rank,
        )
        shard = shaped((UB * half, rank))
        users, keep, give = call(
            user_last_kernel, (state, shard, shard),
            *iterate(sides, user_conf, pairs, others), flops=10 ** 6,
        )
        taken = swap(give, "item", 1)
        (user_factors,) = call(
            functools.partial(join_kernel, block), (shaped((UB * block, rank)),), keep, taken
        )

    with jax.named_scope("gather_users"):
        users, tiles = lax.optimization_barrier((users, tiles))
        found = [users, swap(users, "user", 1), swap(users, "user", 2)]

    with jax.named_scope("item_tiles"):
        lists = tiles[:, 2 * slots * block : 2 * slots * block + 2]
        columns = near * row_blocks * block
        item_conf, item_weight = call(
            functools.partial(
                item_tiles_kernel, unobserved / (user_factors.shape[0] * n_user * n_item), row_blocks, slots
            ),
            (shaped((2 * block, columns)), shaped((2 * block, columns), bf16)),
            lists, tiles, scalars=1, flops=10 ** 9,
        )

    with jax.named_scope("gather_users"):
        neighbour, item_conf = lax.optimization_barrier((found[2], item_conf))
        found.append(swap(neighbour, "user", 1))
        marks, ordered = [], []
        for mask, piece in enumerate(found):
            marks += [(mask, True), (mask, False)]
            ordered += [piece, swap(piece, "item", 1)]

    def both(value):
        return value, swap(value, "user", near)

    rows = 2 * block
    with jax.named_scope("item_cg"):
        *sides, pairs = call(
            functools.partial(item_side_kernel, row_blocks, block, marks),
            (shaped((rows // CHUNKS, rank)),) * CHUNKS + (shaped((columns, 2 * rank), bf16),),
            *ordered, item_weight, flops=4 * rows * columns * rank,
        )
        item_factors, unused = call(
            item_last_kernel, (shaped((block, rank)), shaped((rows, rank))),
            *iterate(sides, item_conf, pairs, both), flops=10 ** 6,
        )
    return (user_factors, item_factors)


def fits_dense(mesh):
    n_user, n_item = mesh.shape["user"], mesh.shape["item"]
    block = 128
    user_bytes = UB * n_item * block * n_user * block * 4
    return user_bytes <= DENSE_LIMIT and n_item % 2 == 0 and n_user == 8


def block_sum(slot_terms, block_ids, row_count, block_size):
    block_count = row_count // block_size
    targets = jnp.arange(block_count, dtype=jnp.int32)
    onehot = (block_ids[:, None] == targets[None, :]).astype(jnp.float32)
    summed = jnp.einsum("tr,tik->rik", onehot, slot_terms, precision=highest)
    return summed.reshape(row_count, slot_terms.shape[2])


def group_products(own_blocks, other_blocks, tile_values, own_ids, other_ids):
    own_rows = jnp.take(own_blocks, own_ids, axis=0)
    other_rows = jnp.take(other_blocks, other_ids, axis=0)
    scores = jnp.einsum("tik,tjk->tij", own_rows, other_rows, precision=highest)
    return jnp.einsum("tij,tjk->tik", scores * tile_values, other_rows, precision=highest)


def slot_products(own_blocks, other_blocks, tile_values, own_ids, other_ids):
    return group_products(own_blocks, other_blocks, tile_values, own_ids, other_ids)


def conjugate(right_side, apply_operator):
    solution = jnp.zeros_like(right_side)
    residual = right_side
    direction = right_side
    norm_now = jnp.sum(residual * residual, axis=-1, keepdims=True)
    for iteration in range(CG_ITERS):
        product_vec = apply_operator(direction)
        step_length = norm_now / jnp.sum(direction * product_vec, axis=-1, keepdims=True)
        solution = solution + step_length * direction
        residual = residual - step_length * product_vec
        norm_next = jnp.sum(residual * residual, axis=-1, keepdims=True)
        direction = residual + norm_next / norm_now * direction
        norm_now = norm_next
    return solution


def shards(item_init, tile_rows, tile_cols, tile_count, conf):
    slot_total = tile_rows.shape[-1]
    block_size = conf.shape[-1]
    factor_rank = item_init.shape[1]
    item_devices = lax.axis_size("item")
    user_devices = lax.axis_size("user")
    row_ids = tile_rows.reshape(slot_total)
    col_ids = tile_cols.reshape(slot_total)
    slot_count = tile_count.reshape(())
    counts = conf.reshape(slot_total, block_size, block_size).astype(jnp.float32)
    usable = (jnp.arange(slot_total, dtype=jnp.int32) < slot_count)[:, None, None]
    confidence = jnp.where(usable, counts, 0.0)
    weights = jnp.where(usable & (counts > 0.0), 1.0 + counts, 0.0)
    user_rows = UB * block_size
    item_rows = IB * block_size
    item_shard = lax.all_gather(item_init, "user", axis=0, tiled=True)
    item_blocks = item_shard.reshape(-1, block_size, factor_rank)
    item_gram = lax.psum(jnp.dot(item_init.T, item_init, precision=highest), ("user", "item"))
    user_weight = unobserved / (item_init.shape[0] * user_devices * item_devices)
    user_terms = jnp.einsum(
        "tij,tjk->tik", weights, jnp.take(item_blocks, col_ids, axis=0), precision=highest
    )
    user_side = lax.psum_scatter(
        block_sum(user_terms, row_ids, user_rows * lax.axis_size("item"), block_size),
        "item",
        scatter_dimension=0,
        tiled=True,
    )

    def user_operator(direction):
        shard_direction = lax.all_gather(direction, "item", axis=0, tiled=True)
        slot_terms = slot_products(
            shard_direction.reshape(-1, block_size, factor_rank),
            item_blocks,
            confidence,
            row_ids,
            col_ids,
        )
        summed = lax.psum_scatter(
            block_sum(slot_terms, row_ids, user_rows * lax.axis_size("item"), block_size),
            "item",
            scatter_dimension=0,
            tiled=True,
        )
        return (
            summed
            + user_weight * jnp.dot(direction, item_gram, precision=highest)
            + ridge * direction
        )

    user_factors = conjugate(user_side, user_operator)
    user_shard = lax.all_gather(user_factors, "item", axis=0, tiled=True)
    user_blocks = user_shard.reshape(-1, block_size, factor_rank)
    user_gram = lax.psum(jnp.dot(user_factors.T, user_factors, precision=highest), ("user", "item"))
    item_weight = unobserved / (user_factors.shape[0] * user_devices * item_devices)
    confidence_cols = jnp.swapaxes(confidence, 1, 2)
    slot_users = jnp.take(user_blocks, row_ids, axis=0)
    item_terms = jnp.einsum("tij,tik->tjk", weights, slot_users, precision=highest)
    item_side = lax.psum_scatter(
        block_sum(item_terms, col_ids, item_rows * lax.axis_size("user"), block_size),
        "user",
        scatter_dimension=0,
        tiled=True,
    )

    def item_operator(direction):
        shard_direction = lax.all_gather(direction, "user", axis=0, tiled=True)
        slot_terms = slot_products(
            shard_direction.reshape(-1, block_size, factor_rank),
            user_blocks,
            confidence_cols,
            col_ids,
            row_ids,
        )
        summed = lax.psum_scatter(
            block_sum(slot_terms, col_ids, item_rows * lax.axis_size("user"), block_size),
            "user",
            scatter_dimension=0,
            tiled=True,
        )
        return (
            summed
            + item_weight * jnp.dot(direction, user_gram, precision=highest)
            + ridge * direction
        )

    item_factors = conjugate(item_side, item_operator)
    return (user_factors, item_factors)


def solution(mesh):
    in_specs = (
        P(("item", "user"), None),
        P("user", "item", None),
        P("user", "item", None),
        P("user", "item"),
        P("user", "item", None, None, None),
    )
    out_specs = (P(("user", "item"), None), P(("item", "user"), None))
    program = dense_shards if fits_dense(mesh) else shards
    return jax.shard_map(program, mesh=mesh, in_specs=in_specs, out_specs=out_specs, check_vma=False)
```

```python
import functools
import math

import jax
import jax.numpy as jnp
from jax import lax
from jax.experimental import pallas as pl
from jax.experimental.pallas import tpu as pltpu
from jax.sharding import PartitionSpec as P

UB = 2
IB = 1
CG_ITERS = 3
CHUNKS = 2


highest = lax.Precision.HIGHEST
ridge = 5.0
unobserved = 256.0

f32 = jnp.float32
bf16 = jnp.bfloat16
MIB = 1 << 20
DENSE_LIMIT = 8 * MIB


def pair(value):
    high = value.astype(bf16)
    low = (value - high.astype(f32)).astype(bf16)
    return high, low


def row_sum(value):
    return jnp.sum(value, axis=-1, keepdims=True)


def split_rows(value):
    high, low = pair(value)
    return jnp.concatenate(
        [jnp.concatenate([high, low], axis=1), jnp.concatenate([low, high], axis=1)], axis=0
    )


def scores_of(lhs, factors):
    rows = lhs.shape[0] // 2
    both = lax.dot_general(lhs, factors, (((1,), (1,)), ((), ())), preferred_element_type=f32)
    return both[:rows] + both[rows:]


def tile_terms(direction, conf_ref, pairs_ref, width, begin):
    rows, rank = direction.shape
    lhs = split_rows(direction)
    total = jnp.zeros((rows, rank), f32)
    for start in range(0, conf_ref.shape[1], width):
        factors = pairs_ref[start : start + width, :]
        weighted = scores_of(lhs, factors) * conf_ref[begin : begin + rows, start : start + width]
        high, low = pair(weighted)
        out = jnp.dot(jnp.concatenate([high, low], axis=0), factors, preferred_element_type=f32)
        total = total + (
            (out[:rows, :rank] + out[:rows, rank:]) + (out[rows:, :rank] + out[rows:, rank:])
        )
    return total


def tile_squares(direction, conf_ref, pairs_ref, width, begin):
    rows, rank = direction.shape
    lhs = split_rows(direction)
    total = jnp.zeros((rows, rank), f32)
    for start in range(0, conf_ref.shape[1], width):
        scores = scores_of(lhs, pairs_ref[start : start + width, :])
        squares = scores * scores * conf_ref[begin : begin + rows, start : start + width]
        for part in range(0, width, rank):
            total = total + squares[:, part : part + rank]
    return total


def write_sides(weight_ref, pairs_ref, side_refs):
    rank = pairs_ref.shape[1] // 2
    both = jnp.dot(weight_ref[...], pairs_ref[...], preferred_element_type=f32)
    start = 0
    for side_ref in side_refs:
        rows = slice(start, start + side_ref.shape[0])
        side_ref[...] = both[rows, :rank] + both[rows, rank:]
        start += side_ref.shape[0]


def advance(solution, residual, direction, product):
    norm_now = row_sum(residual * residual)
    step_length = norm_now / row_sum(direction * product)
    solution = solution + step_length * direction
    residual = residual - step_length * product
    direction = residual + row_sum(residual * residual) / norm_now * direction
    return solution, residual, direction


def pack_kernel(slots, ids_ref, conf_ref, named_ref, given_ref, send_ref, held, in_sems, sems):
    slot_total, block, _ = conf_ref.shape
    half = block // 2
    owners = slot_total // slots
    near = owners // 2
    core = lax.rem(lax.axis_index("item"), 2)
    taken = [
        pltpu.make_async_copy(conf_ref.at[slot], held.at[slot], in_sems.at[slot]) for slot in range(slot_total)
    ]
    for copy in taken:
        copy.start()
    rows = pl.ds(pl.multiple_of((1 - core) * half, half), half)
    copies = []
    for owner in range(near):
        target = send_ref.at[owner, 2 * slots * block :, :]
        copies.append(pltpu.make_async_copy(named_ref, target, sems.at[len(copies)]))
        copies[-1].start()
    for slot in range(slot_total):
        owner = lax.rem(ids_ref[1, 0] + slot, owners)
        start = pl.multiple_of((owner // near * slots + slot // owners) * block, block)
        target = send_ref.at[lax.rem(owner, near), pl.ds(start, block), :]
        taken[slot].wait()
        copies.append(pltpu.make_async_copy(held.at[slot], target, sems.at[len(copies)]))
        copies[-1].start()
        if (slot + 1) % owners == 0:
            slots_in = pl.ds(slot + 1 - owners, owners)
            part = pltpu.make_async_copy(
                held.at[slots_in, rows, :], given_ref.at[slots_in], sems.at[len(copies)]
            )
            copies.append(part)
            part.start()
    for copy in copies:
        copy.wait()


def user_tile(named_ref, slot, base, counts, dense_ref, weight_ref):
    half, block = counts.shape
    owners = dense_ref.shape[1] // block // 2
    owner = lax.rem(named_ref[1, 0] + slot, owners)
    row = pl.multiple_of(named_ref[0, slot] * half, half)
    col = pl.multiple_of((base + jnp.bitwise_xor(owner, lax.axis_index("user"))) * block, block)
    at = (pl.ds(row, half), pl.ds(col, block))
    value = counts.astype(f32)
    dense_ref[at] = dense_ref[at] + value
    weight_ref[at] = weight_ref[at] + jnp.where(value > 0.0, 1.0 + value, 0.0).astype(bf16)


def own_tiles_kernel(weight_zero, named_ref, conf_ref, dense_ref, weight_ref, held, sem):
    slot_total, block, _ = conf_ref.shape
    half = block // 2
    core = lax.rem(lax.axis_index("item"), 2)
    rows = pl.ds(pl.multiple_of(core * half, half), half)
    step = slot_total // sem.shape[0]
    copies = []
    for place in range(sem.shape[0]):
        slots = pl.ds(place * step, step)
        copies.append(pltpu.make_async_copy(conf_ref.at[slots, rows, :], held.at[slots], sem.at[place]))
        copies[-1].start()
    dense_ref[...] = jnp.full(dense_ref.shape, weight_zero, f32)
    weight_ref[...] = jnp.zeros(weight_ref.shape, bf16)
    for slot in range(slot_total):
        if slot % step == 0:
            copies[slot // step].wait()
        counts = jnp.where(slot < named_ref[1, 1], held[slot], 0)
        user_tile(named_ref, slot, 0, counts, dense_ref, weight_ref)


def other_tiles_kernel(named_ref, half_ref, dense_in, weight_in, dense_ref, weight_ref):
    slot_total, _, block = half_ref.shape
    owners = dense_ref.shape[1] // block // 2

    for slot in range(slot_total):
        counts = jnp.where(slot < named_ref[1, 1], half_ref[slot], 0)
        user_tile(named_ref, slot, owners, counts, dense_ref, weight_ref)


def user_side_kernel(count, *refs):
    pieces, (weight_ref, *side_refs, pairs_ref) = refs[:count], refs[count:]
    block = pairs_ref.shape[0] // count
    for place, piece in enumerate(pieces):
        high, low = pair(piece[:block, :])
        pairs_ref[place * block : (place + 1) * block, :] = jnp.concatenate([high, low], axis=1)
    write_sides(weight_ref, pairs_ref, side_refs)


def first_kernel(width, begin, own_ref, other_ref, conf_ref, pairs_ref, side_ref, out_ref):
    side = own_ref[...] + other_ref[...]
    side_ref[...] = side
    out_ref[...] = tile_terms(side, conf_ref, pairs_ref, width, begin)


def second_kernel(
    width, begin, side_ref, own_ref, other_ref, conf_ref, pairs_ref, x_ref, r_ref, d_ref, out_ref
):
    side = side_ref[...]
    product = own_ref[...] + other_ref[...] + ridge * side
    x, r, d = advance(jnp.zeros_like(side), side, side, product)
    x_ref[...] = x
    r_ref[...] = r
    d_ref[...] = d
    out_ref[...] = tile_terms(d, conf_ref, pairs_ref, width, begin)


def third_kernel(
    width, begin, x_in, r_in, d_in, own_ref, other_ref, conf_ref, pairs_ref, x_ref, r_ref, d_ref, sums_ref
):
    direction = d_in[...]
    product = own_ref[...] + other_ref[...] + ridge * direction
    x, r, d = advance(x_in[...], r_in[...], direction, product)
    x_ref[...] = x
    r_ref[...] = r
    d_ref[...] = d
    squares = tile_squares(d, conf_ref, pairs_ref, width, begin)
    ones = jnp.ones((8, squares.shape[1]), bf16)
    sums = jnp.zeros(sums_ref.shape, f32)
    for unused in range(3):
        part = squares.astype(bf16)
        squares = squares - part.astype(f32)
        sums = sums + lax.dot_general(ones, part, (((1,), (1,)), ((), ())), preferred_element_type=f32)
    sums_ref[...] = sums


def solve(refs, out_ref):
    start = 0
    for place in range(0, len(refs), 5):
        x_in, r_in, d_in, own_ref, other_ref = refs[place : place + 5]
        residual, direction = r_in[...], d_in[...]
        sums = jnp.transpose(own_ref[...] + other_ref[...])[:, :1]
        length = row_sum(residual * residual) / (sums + ridge * row_sum(direction * direction))
        out_ref[start : start + residual.shape[0], :] = x_in[...] + length * direction
        start += residual.shape[0]


def user_last_kernel(*refs):
    out_ref, keep_ref, give_ref = refs[-3:]
    solve(refs[:-3], out_ref)
    place = lax.axis_index("item")
    rows = keep_ref.shape[0]
    keep_ref[...] = out_ref[pl.ds(pl.multiple_of(place * rows, rows), rows), :]
    other = jnp.bitwise_xor(place, 1)
    give_ref[...] = out_ref[pl.ds(pl.multiple_of(other * rows, rows), rows), :]


def item_tiles_kernel(weight_zero, row_blocks, slots, lists_ref, tiles_ref, dense_ref, weight_ref):
    near = tiles_ref.shape[0]
    block = tiles_ref.shape[2]
    me = lax.rem(lax.axis_index("user"), near)
    dense_ref[...] = jnp.full(dense_ref.shape, weight_zero, f32)
    weight_ref[...] = jnp.zeros(weight_ref.shape, bf16)
    for source in range(near):
        mask = jnp.bitwise_xor(source, me)
        for upper in range(2):
            first = lax.rem(me + upper * near - lists_ref[source, 1, 0] + 2 * near, 2 * near)
            for slot in range(slots):
                start = (upper * slots + slot) * block
                place = first + 2 * near * slot
                used = place < lists_ref[source, 1, 1]
                tile = jnp.where(used, tiles_ref[source, start : start + block, :], 0)
                value = jnp.transpose(tile.astype(f32))
                row = lists_ref[source, 0, place]
                col = pl.multiple_of((mask * row_blocks + row) * block, block)
                at = (slice(upper * block, (upper + 1) * block), pl.ds(col, block))
                dense_ref[at] = dense_ref[at] + value
                weight_ref[at] = weight_ref[at] + jnp.where(value > 0.0, 1.0 + value, 0.0).astype(bf16)


def join_kernel(block, own_ref, other_ref, out_ref):
    half = block // 2
    core = lax.rem(lax.axis_index("item"), 2)
    for start in range(0, out_ref.shape[0], block):
        for offset, part_ref in ((core, own_ref), (1 - core, other_ref)):
            rows = pl.ds(pl.multiple_of(start + offset * half, half), half)
            out_ref[rows, :] = part_ref[start // 2 : start // 2 + half, :]


def item_side_kernel(row_blocks, block, marks, *refs):
    pieces, (weight_ref, *side_refs, pairs_ref) = refs[: len(marks)], refs[len(marks) :]
    half = block // 2
    core = lax.rem(lax.axis_index("item"), 2)
    for (mask, own_half), piece in zip(marks, pieces):
        offset = pl.multiple_of((core if own_half else 1 - core) * half, half)
        for row in range(row_blocks):
            high, low = pair(piece[row * half : (row + 1) * half, :])
            start = (mask * row_blocks + row) * block
            pairs_ref[pl.ds(start + offset, half), :] = jnp.concatenate([high, low], axis=1)
    write_sides(weight_ref, pairs_ref, side_refs)


def item_last_kernel(*refs):
    out_ref, all_ref = refs[-2:]
    solve(refs[:-2], all_ref)
    rows = out_ref.shape[0]
    upper = lax.axis_index("user") // (lax.axis_size("user") // 2)
    out_ref[...] = all_ref[pl.ds(pl.multiple_of(upper * rows, rows), rows), :]


VMEM = pltpu.VMEM
SMEM = pltpu.SMEM


def call(kernel, outs, *operands, scalars=0, far=0, far_outs=0, flops=0, scratch=(), limit=16, aliases=None):
    size = sum(op.size * op.dtype.itemsize for op in operands)
    size += sum(4 * math.prod(out.shape) for out in outs)
    spaces = [SMEM] * scalars + [pl.ANY] * far + [VMEM] * (len(operands) - scalars - far)
    return pl.pallas_call(
        kernel,
        out_shape=tuple(outs),
        in_specs=[pl.BlockSpec(memory_space=space) for space in spaces],
        out_specs=tuple(pl.BlockSpec(memory_space=pl.ANY if place < far_outs else VMEM) for place in range(len(outs))),
        scratch_shapes=scratch,
        input_output_aliases=aliases or {},
        compiler_params=pltpu.CompilerParams(vmem_limit_bytes=limit * MIB),
        cost_estimate=pl.CostEstimate(flops=flops, bytes_accessed=size, transcendentals=0),
    )(*operands)


def shaped(shape, dtype=f32):
    return jax.ShapeDtypeStruct(shape, dtype)


def dense_shards(item_init, tile_rows, tile_cols, tile_count, conf):
    slot_total = tile_rows.shape[-1]
    block, rank = conf.shape[-1], item_init.shape[1]
    half = block // 2
    n_item, n_user = lax.axis_size("item"), lax.axis_size("user")
    row_blocks = UB * n_item
    rows = row_blocks * half
    slots = -(-slot_total // n_user)
    width = 4 * rank
    def swap(value, axis, mask):
        size = n_item if axis == "item" else n_user
        return lax.ppermute(value, axis, [(place, place ^ mask) for place in range(size)])

    def others(value):
        total = value
        mask = 2
        while mask < n_item:
            moved = swap(total, "item", mask)
            if mask * 2 >= n_item:
                return total, moved
            total = total + moved
            mask *= 2

    conf = conf.reshape(slot_total, block, block)
    def after(value, *tokens):
        return lax.optimization_barrier((value, *tokens))[0]

    named = sum(
        jnp.pad(value.reshape(1, -1), ((row, 7 - row), (lane, rank - lane - size)))
        for value, row, lane, size in (
            (tile_rows, 0, 0, slot_total), (tile_cols[..., :1], 1, 0, 1), (tile_count, 1, 1, 1)
        )
    )
    near = n_user // 2
    with jax.named_scope("gather_items"):
        pieces = {0: item_init}
        for mask in (6, 4, 2, 1):
            pieces[mask] = swap(item_init, "user", mask)

    with jax.named_scope("gather_items"):
        for mask in (2, 6, 4):
            pieces[mask + 1] = swap(after(pieces[mask], named), "user", 1)
        own_items = [pieces[mask] for mask in range(n_user)]
        other_items = [swap(piece, "item", 1) for piece in own_items]

    with jax.named_scope("pack_tiles"):
        far_conf = pltpu.with_memory_space_constraint(conf, pltpu.HBM)
        given, packed = call(
            functools.partial(pack_kernel, slots),
            (
                pltpu.HBM((slot_total, half, block), jnp.int32),
                pltpu.HBM((near, 2 * slots * block + 8, block), jnp.int32),
            ),
            after(named, pieces[3]), far_conf, named, scalars=1, far=1, far_outs=2, limit=16,
            scratch=(
                pltpu.VMEM(conf.shape, jnp.int32),
                pltpu.SemaphoreType.DMA((slot_total,)),
                pltpu.SemaphoreType.DMA((slot_total + slots + near,)),
            ),
        )
        other_named = swap(named, "item", 1)
        other_half = swap(given, "item", 1)

    with jax.named_scope("send_tiles"):
        halves = [list(range(start, start + near)) for start in (0, near)]
        tiles = lax.all_to_all(
            after(packed, *own_items), "user", 0, 0, tiled=True, axis_index_groups=halves
        )
        own_named = after(named, *own_items)

    with jax.named_scope("user_tiles"):
        columns = 2 * n_user * block
        dense = (shaped((rows, columns)), shaped((rows, columns), bf16))
        user_conf, user_weight = call(
            functools.partial(own_tiles_kernel, unobserved / (item_init.shape[0] * n_user * n_item)),
            dense, own_named, far_conf, scalars=1, far=1, flops=10 ** 9,
            scratch=(pltpu.VMEM((slot_total, half, block), jnp.int32), pltpu.SemaphoreType.DMA((8,))),
        )
        user_conf, user_weight = call(
            other_tiles_kernel, dense, other_named, other_half, user_conf, user_weight,
            scalars=1, flops=10 ** 9, aliases={2: 0, 3: 1},
        )

    def iterate(sides, confidence, pairs, both):
        work = 2 * sides[0].shape[0] * pairs.shape[0] * rank
        states = []
        for place, part in enumerate(sides):
            size = part.shape[0]
            state, begin = shaped(part.shape), place * size
            side, part = call(
                functools.partial(first_kernel, width, begin), (state, state),
                *both(part), confidence, pairs, flops=6 * work,
            )
            states.append((begin, state, (side,), part))
        for kernel in (second_kernel, third_kernel):
            for place, (begin, state, carried, part) in enumerate(states):
                last = shaped((8, state.shape[0])) if kernel is third_kernel else state
                *carried, part = call(
                    functools.partial(kernel, width, begin), (state, state, state, last),
                    *carried, *both(part), confidence, pairs, flops=6 * work,
                )
                states[place] = (begin, state, carried, part)
        return [value for _, _, carried, sums in states for value in (*carried, *both(sums))]

    state = shaped((rows, rank))
    with jax.named_scope("user_cg"):
        *sides, pairs = call(
            functools.partial(user_side_kernel, 2 * n_user),
            (shaped((rows // CHUNKS, rank)),) * CHUNKS + (shaped((columns, 2 * rank), bf16),),
            *own_items, *other_items, user_weight, flops=4 * rows * columns * rank,
        )
        shard = shaped((UB * half, rank))
        users, keep, give = call(
            user_last_kernel, (state, shard, shard),
            *iterate(sides, user_conf, pairs, others), flops=10 ** 6,
        )
        taken = swap(give, "item", 1)
        (user_factors,) = call(
            functools.partial(join_kernel, block), (shaped((UB * block, rank)),), keep, taken
        )

    with jax.named_scope("gather_users"):
        users, tiles = lax.optimization_barrier((users, tiles))
        found = [users, swap(users, "user", 1), swap(users, "user", 2)]

    with jax.named_scope("item_tiles"):
        lists = tiles[:, 2 * slots * block : 2 * slots * block + 2]
        columns = near * row_blocks * block
        item_conf, item_weight = call(
            functools.partial(
                item_tiles_kernel, unobserved / (user_factors.shape[0] * n_user * n_item), row_blocks, slots
            ),
            (shaped((2 * block, columns)), shaped((2 * block, columns), bf16)),
            lists, tiles, scalars=1, flops=10 ** 9,
        )

    with jax.named_scope("gather_users"):
        neighbour, item_conf = lax.optimization_barrier((found[2], item_conf))
        found.append(swap(neighbour, "user", 1))
        marks, ordered = [], []
        for mask, piece in enumerate(found):
            marks += [(mask, True), (mask, False)]
            ordered += [piece, swap(piece, "item", 1)]

    def both(value):
        return value, swap(value, "user", near)

    rows = 2 * block
    with jax.named_scope("item_cg"):
        *sides, pairs = call(
            functools.partial(item_side_kernel, row_blocks, block, marks),
            (shaped((rows // CHUNKS, rank)),) * CHUNKS + (shaped((columns, 2 * rank), bf16),),
            *ordered, item_weight, flops=4 * rows * columns * rank,
        )
        item_factors, unused = call(
            item_last_kernel, (shaped((block, rank)), shaped((rows, rank))),
            *iterate(sides, item_conf, pairs, both), flops=10 ** 6,
        )
    return (user_factors, item_factors)


def fits_dense(mesh):
    n_user, n_item = mesh.shape["user"], mesh.shape["item"]
    block = 128
    user_bytes = UB * n_item * block * n_user * block * 4
    return user_bytes <= DENSE_LIMIT and n_item % 2 == 0 and n_user == 8


def block_sum(slot_terms, block_ids, row_count, block_size):
    block_count = row_count // block_size
    targets = jnp.arange(block_count, dtype=jnp.int32)
    onehot = (block_ids[:, None] == targets[None, :]).astype(jnp.float32)
    summed = jnp.einsum("tr,tik->rik", onehot, slot_terms, precision=highest)
    return summed.reshape(row_count, slot_terms.shape[2])


def group_products(own_blocks, other_blocks, tile_values, own_ids, other_ids):
    own_rows = jnp.take(own_blocks, own_ids, axis=0)
    other_rows = jnp.take(other_blocks, other_ids, axis=0)
    scores = jnp.einsum("tik,tjk->tij", own_rows, other_rows, precision=highest)
    return jnp.einsum("tij,tjk->tik", scores * tile_values, other_rows, precision=highest)


def slot_products(own_blocks, other_blocks, tile_values, own_ids, other_ids):
    return group_products(own_blocks, other_blocks, tile_values, own_ids, other_ids)


def conjugate(right_side, apply_operator):
    solution = jnp.zeros_like(right_side)
    residual = right_side
    direction = right_side
    norm_now = jnp.sum(residual * residual, axis=-1, keepdims=True)
    for iteration in range(CG_ITERS):
        product_vec = apply_operator(direction)
        step_length = norm_now / jnp.sum(direction * product_vec, axis=-1, keepdims=True)
        solution = solution + step_length * direction
        residual = residual - step_length * product_vec
        norm_next = jnp.sum(residual * residual, axis=-1, keepdims=True)
        direction = residual + norm_next / norm_now * direction
        norm_now = norm_next
    return solution


def shards(item_init, tile_rows, tile_cols, tile_count, conf):
    slot_total = tile_rows.shape[-1]
    block_size = conf.shape[-1]
    factor_rank = item_init.shape[1]
    item_devices = lax.axis_size("item")
    user_devices = lax.axis_size("user")
    row_ids = tile_rows.reshape(slot_total)
    col_ids = tile_cols.reshape(slot_total)
    slot_count = tile_count.reshape(())
    counts = conf.reshape(slot_total, block_size, block_size).astype(jnp.float32)
    usable = (jnp.arange(slot_total, dtype=jnp.int32) < slot_count)[:, None, None]
    confidence = jnp.where(usable, counts, 0.0)
    weights = jnp.where(usable & (counts > 0.0), 1.0 + counts, 0.0)
    user_rows = UB * block_size
    item_rows = IB * block_size
    item_shard = lax.all_gather(item_init, "user", axis=0, tiled=True)
    item_blocks = item_shard.reshape(-1, block_size, factor_rank)
    item_gram = lax.psum(jnp.dot(item_init.T, item_init, precision=highest), ("user", "item"))
    user_weight = unobserved / (item_init.shape[0] * user_devices * item_devices)
    user_terms = jnp.einsum(
        "tij,tjk->tik", weights, jnp.take(item_blocks, col_ids, axis=0), precision=highest
    )
    user_side = lax.psum_scatter(
        block_sum(user_terms, row_ids, user_rows * lax.axis_size("item"), block_size),
        "item",
        scatter_dimension=0,
        tiled=True,
    )

    def user_operator(direction):
        shard_direction = lax.all_gather(direction, "item", axis=0, tiled=True)
        slot_terms = slot_products(
            shard_direction.reshape(-1, block_size, factor_rank),
            item_blocks,
            confidence,
            row_ids,
            col_ids,
        )
        summed = lax.psum_scatter(
            block_sum(slot_terms, row_ids, user_rows * lax.axis_size("item"), block_size),
            "item",
            scatter_dimension=0,
            tiled=True,
        )
        return (
            summed
            + user_weight * jnp.dot(direction, item_gram, precision=highest)
            + ridge * direction
        )

    user_factors = conjugate(user_side, user_operator)
    user_shard = lax.all_gather(user_factors, "item", axis=0, tiled=True)
    user_blocks = user_shard.reshape(-1, block_size, factor_rank)
    user_gram = lax.psum(jnp.dot(user_factors.T, user_factors, precision=highest), ("user", "item"))
    item_weight = unobserved / (user_factors.shape[0] * user_devices * item_devices)
    confidence_cols = jnp.swapaxes(confidence, 1, 2)
    slot_users = jnp.take(user_blocks, row_ids, axis=0)
    item_terms = jnp.einsum("tij,tik->tjk", weights, slot_users, precision=highest)
    item_side = lax.psum_scatter(
        block_sum(item_terms, col_ids, item_rows * lax.axis_size("user"), block_size),
        "user",
        scatter_dimension=0,
        tiled=True,
    )

    def item_operator(direction):
        shard_direction = lax.all_gather(direction, "user", axis=0, tiled=True)
        slot_terms = slot_products(
            shard_direction.reshape(-1, block_size, factor_rank),
            user_blocks,
            confidence_cols,
            col_ids,
            row_ids,
        )
        summed = lax.psum_scatter(
            block_sum(slot_terms, col_ids, item_rows * lax.axis_size("user"), block_size),
            "user",
            scatter_dimension=0,
            tiled=True,
        )
        return (
            summed
            + item_weight * jnp.dot(direction, user_gram, precision=highest)
            + ridge * direction
        )

    item_factors = conjugate(item_side, item_operator)
    return (user_factors, item_factors)


def solution(mesh):
    in_specs = (
        P(("item", "user"), None),
        P("user", "item", None),
        P("user", "item", None),
        P("user", "item"),
        P("user", "item", None, None, None),
    )
    out_specs = (P(("user", "item"), None), P(("item", "user"), None))
    program = dense_shards if fits_dense(mesh) else shards
    return jax.shard_map(program, mesh=mesh, in_specs=in_specs, out_specs=out_specs, check_vma=False)
```
